32 devices in a mesh: items: 8 (over z, y), rep: 4 (over x, core).
Axes of the slice: x: 2, y: 2, z: 4, core: 2. Of those that a mesh axis runs over, the one named last changes fastest.
Arguments:
- embeds: bfloat16 [8192, 256], P(('items', 'rep')), may hold values from -6 to 6
- assign: int32 [8192], P(('items', 'rep')), may hold values from 0 to 4095, as said below
- list_slot: int32 [4096], replicated, may hold values from 0 to 4095, as said below
- old_centroids: bfloat16 [4096, 256], P('items'), may hold values from -6 to 6
Outputs:
- new_centroids: bfloat16 [4096, 256], P('items')
- codes: bfloat16 [8, 4, 1024, 256], P('items', 'rep')
- row_scales: float32 [8, 4, 1024], P('items', 'rep')
The draws below stay inside these ranges and needn't reach their ends.
Inputs may be any that keep to these rules, and one draw needn't show every extreme that they name: `assign`: on one device at most 128 items go to lists of one owner, and some owner receives exactly 128 items from every device. `list_slot`: A permutation of the lists.
All inputs are finite; a program needn't handle non-finite values. Where the reference program divides by a largest or mean magnitude, that divisor is 1e-20 or more.
Results may differ from the reference program's by a relative error of at most 0.0041.
Values may be sent and summed in bfloat16 or wider, within the bound.
No kernel may reach another device: no remote copies, remote signals or barrier semaphores. Data moves between devices by JAX's collectives and lax.ppermute only.
A program may use at most 64 MiB of HBM per device.

```python
import jax
import jax.numpy as jnp
from jax import lax

D = 256
LIST_DEV = 512
ITEM_DEV = 256
NLIST = 4096
ITEMS = 8192
CAP = 128
N_ITEMS = 8
N_REP = 4


def slot_table(key):
    return jax.random.permutation(jax.random.fold_in(key, 11), NLIST).astype(jnp.int32)


def draw_list_slot(key, part):
    return slot_table(key)


def draw_assign(key, part):
    table = slot_table(key)
    inverse = jnp.zeros((NLIST,), jnp.int32).at[table].set(jnp.arange(NLIST, dtype=jnp.int32))
    blocks = N_ITEMS * N_REP
    heavy = jax.random.randint(jax.random.fold_in(key, 12), (), 0, N_ITEMS).astype(jnp.int32)
    offsets = jax.random.randint(jax.random.fold_in(key, 13), (blocks, ITEM_DEV), 0, 2).astype(jnp.int32)
    rotate = jax.random.randint(jax.random.fold_in(key, 14), (blocks, 1), 0, N_ITEMS - 1).astype(jnp.int32)
    position = jnp.arange(ITEM_DEV, dtype=jnp.int32)[None, :]
    others = (position - CAP + offsets + rotate) % (N_ITEMS - 1)
    others = others + (others >= heavy).astype(jnp.int32)
    owners = jnp.where(position < CAP, heavy, others)
    shuffle_keys = jax.random.split(jax.random.fold_in(key, 15), blocks)
    shuffle = jax.vmap(lambda k: jax.random.permutation(k, ITEM_DEV))(shuffle_keys)
    owners = jnp.take_along_axis(owners, shuffle, axis=1)
    local = jax.random.randint(jax.random.fold_in(key, 16), (blocks, ITEM_DEV), 0, LIST_DEV).astype(jnp.int32)
    return inverse[(owners * LIST_DEV + local).reshape(-1)]


def steps_of(stream_key, shape, cuts, least, top_value):
    factor_of = 1.0
    for axis_at, parts in cuts:
        heights = jax.random.uniform(jax.random.fold_in(jax.random.fold_in(stream_key, 6), axis_at), (parts,), jnp.float32, least / len(cuts), top_value / len(cuts))
        factor_of = factor_of * jnp.repeat(jnp.exp(heights), shape[axis_at] // parts).reshape((-1,) + (1,) * (len(shape) - 1 - axis_at))
    return factor_of


def gaussian(key, shape, width, reach, cuts=(), kind=jnp.bfloat16):
    array = width * jax.random.normal(key, shape, jnp.float32)
    if cuts:
        array = array * steps_of(key, shape, cuts, -0.22, 0.18)
    return jnp.clip(array, -reach, reach).astype(kind)


def setup_inputs(seed: int = 0) -> dict:
    arg_keys = jax.random.split(jax.random.key(seed), 5)
    return {
        "embeds": gaussian(arg_keys[0], (ITEMS, D), 1.0, 6.0, ((0, 32),)),
        "assign": draw_assign(jax.random.fold_in(arg_keys[4], 71), 0),
        "list_slot": draw_list_slot(jax.random.fold_in(arg_keys[4], 71), 0),
        "old_centroids": gaussian(arg_keys[3], (NLIST, D), 1.0, 6.0, ((0, 8),)),
    }


def reference(embeds, assign, list_slot, old_centroids):
    slot = list_slot[assign]
    owner = slot // LIST_DEV
    sums = jax.ops.segment_sum(embeds.astype(jnp.float32), slot, NLIST)
    counts = jax.ops.segment_sum(jnp.ones(slot.shape, jnp.float32), slot, NLIST)
    fresh = ((sums + old_centroids.astype(jnp.float32)) / (counts + 1.0)[:, None]).astype(jnp.bfloat16)
    blocks = N_ITEMS * N_REP

    def ranks(row):
        member = (row[:, None] == jnp.arange(N_ITEMS, dtype=jnp.int32)[None, :]).astype(jnp.int32)
        return jnp.sum(member * (jnp.cumsum(member, axis=0) - 1), axis=1)

    rank = lax.map(ranks, owner.reshape(blocks, ITEM_DEV)).reshape(-1)
    block = jnp.arange(ITEMS, dtype=jnp.int32) // ITEM_DEV
    source = block // N_REP
    split = block % N_REP
    place = (owner * N_REP + split) * (N_ITEMS * CAP) + source * CAP + rank

    def quantize(pair):
        rows, slots = pair
        residual = rows.astype(jnp.float32) - fresh[slots].astype(jnp.float32)
        amax = jnp.max(jnp.abs(residual), axis=1)
        coded = (residual * (127.0 / (amax + 1e-6))[:, None]).astype(jnp.bfloat16)
        return coded, amax / 127.0

    coded, scales = lax.map(quantize, (embeds.reshape(blocks, ITEM_DEV, D), slot.reshape(blocks, ITEM_DEV)))
    total = N_ITEMS * N_REP * N_ITEMS * CAP
    codes = jnp.zeros((total, D), jnp.bfloat16).at[place].set(coded.reshape(-1, D))
    row_scales = jnp.zeros((total,), jnp.float32).at[place].set(scales.reshape(-1))
    return (fresh, codes.reshape(N_ITEMS, N_REP, N_ITEMS * CAP, D), row_scales.reshape(N_ITEMS, N_REP, N_ITEMS * CAP))
```

```python
import jax
import jax.numpy as jnp
from jax import lax
from jax.experimental import pallas as pl
from jax.experimental.pallas import tpu as pltpu
from jax.sharding import PartitionSpec as P

HEAD = 16
VMEM = pl.BlockSpec(memory_space=pltpu.VMEM)
SMEM = pl.BlockSpec(memory_space=pltpu.SMEM)


def _log2(n):
    return n.bit_length() - 1


def _iota(shape, dim):
    return lax.broadcasted_iota(jnp.int32, shape, dim)


def _slots(table, assign):
    t, n = table.shape[0], assign.shape[1]
    hot = (_iota((t, n), 0) == (assign >> 7)).astype(jnp.float32).astype(jnp.bfloat16)
    lane = _iota((128, n), 0) == (assign & 127)

    def pick(part):
        part = part.astype(jnp.float32).astype(jnp.bfloat16)
        rows = lax.dot_general(
            part, hot, (((0,), (0,)), ((), ())), preferred_element_type=jnp.float32
        )
        return jnp.sum(jnp.where(lane, rows, 0.0), axis=0, keepdims=True)

    return (pick(table & 255) + 256.0 * pick(table >> 8)).astype(jnp.int32)


def _route(sel, lo, hi, rows, outs):
    n = rows.shape[0]
    capacity = outs[0].shape[0] - HEAD
    place = jnp.concatenate(
        [(_iota((capacity, n), 0) == sel[k : k + 1, :]).astype(jnp.float32) for k in range(len(outs))],
        axis=0,
    ).astype(jnp.bfloat16)
    moved = jnp.dot(place, rows, preferred_element_type=jnp.float32).astype(jnp.bfloat16)
    first = _iota((HEAD, n), 0) == 0
    values = jnp.where(first, lo, hi).astype(jnp.bfloat16)
    labels = lax.dot_general(
        values, place, (((1,), (1,)), ((), ())), preferred_element_type=jnp.float32
    )
    for k, out in enumerate(outs):
        part = labels[:, k * capacity : (k + 1) * capacity]
        head = jnp.concatenate([part[0:1, :], part[1:2, :]], axis=1)
        out[0:capacity, :] = moved[k * capacity : (k + 1) * capacity, :]
        out[capacity:, :] = jnp.broadcast_to(head, (HEAD, head.shape[1])).astype(jnp.bfloat16)


def _route_own_kernel(list_dev, at, own_assign, far_assign, table, rows, o0, o1, o2, o3, far):
    n = own_assign.shape[1]
    me = at[0]
    slot = _slots(table[...], jnp.concatenate([own_assign[...], far_assign[...]], axis=1))
    relative = (slot >> _log2(list_dev)) ^ me
    code = (slot & (list_dev - 1)) + 1
    lo = (code & 255).astype(jnp.float32)
    hi = (code >> 8).astype(jnp.float32)
    member = (_iota((8, 2 * n), 0) == relative).astype(jnp.float32)
    member = jnp.concatenate([member[:, :n], member[:, n:]], axis=0)
    before = (_iota((n, n), 0) < _iota((n, n), 1)).astype(jnp.float32).astype(jnp.bfloat16)
    count = jnp.dot(member.astype(jnp.bfloat16), before, preferred_element_type=jnp.float32)
    sel = jnp.where(member > 0.0, count, -1.0).astype(jnp.int32)
    _route(sel[0:8, :], lo[:, :n], hi[:, :n], rows[...], (o0, o1, o2, o3))
    eight = _iota((8, n), 0)
    far_sel = jnp.where(eight < 4, sel[8:16, :], 0)
    far_sel = jnp.where(eight == 4, lo[:, n:].astype(jnp.int32), far_sel)
    far[...] = jnp.where(eight == 5, hi[:, n:].astype(jnp.int32), far_sel)


def _route_far_kernel(far, rows, o0, o1, o2, o3):
    lo = far[4:5, :].astype(jnp.float32)
    hi = far[5:6, :].astype(jnp.float32)
    _route(far[...], lo, hi, rows[...], (o0, o1, o2, o3))


def _labels(block):
    capacity = block.shape[0] - HEAD
    head = block[capacity:, :].astype(jnp.float32)[0:1, :]
    return (head[:, :capacity] + 256.0 * head[:, capacity:]).astype(jnp.int32) - 1


def _sums_kernel(at, *refs):
    blocks, (send, keep) = refs[:8], refs[8:]
    half = send.shape[0] - 8
    capacity = blocks[0].shape[0] - HEAD
    rows = jnp.concatenate([b[0:capacity, :] for b in blocks], axis=0)
    labels = jnp.concatenate([_labels(b) for b in blocks], axis=1)
    ones = jnp.ones((16, rows.shape[0]), jnp.bfloat16)
    for out, side in ((send, 1 - at[1]), (keep, at[1])):
        hot = (_iota((half, rows.shape[0]), 0) + side * half == labels).astype(jnp.float32)
        hot = hot.astype(jnp.bfloat16)
        out[0:half, :] = jnp.dot(hot, rows, preferred_element_type=jnp.float32)
        out[half:, :] = lax.dot_general(
            ones, hot, (((1,), (1,)), ((), ())), preferred_element_type=jnp.float32
        )[0:8, :]


def _fresh_kernel(at, part, got, old, out):
    half = out.shape[0]
    total = part[...] + got[...]
    counts = jnp.sum(
        jnp.where(_iota((half, half), 0) == _iota((half, half), 1), total[half : half + 1, :], 0.0),
        axis=1,
        keepdims=True,
    )
    mine = old[pl.ds(pl.multiple_of(at[1] * half, half), half), :].astype(jnp.float32)
    out[...] = ((total[:half, :] + mine) / (counts + 1.0)).astype(jnp.bfloat16)


def _codes_kernel(at, *refs):
    blocks, (mine, other, fresh, codes, scales) = refs[:8], refs[8:]
    half = mine.shape[0]
    capacity = blocks[0].shape[0] - HEAD
    me, side = at[0], at[1]
    fresh[pl.ds(pl.multiple_of(side * half, half), half), :] = mine[...]
    fresh[pl.ds(pl.multiple_of((1 - side) * half, half), half), :] = other[...]
    table = fresh[...]
    eye = _iota((capacity, capacity), 0) == _iota((capacity, capacity), 1)
    for k, block in enumerate(blocks):
        column = jnp.sum(
            jnp.where(eye, _labels(block).astype(jnp.float32), 0.0), axis=1, keepdims=True
        ).astype(jnp.int32)
        hot = (_iota((capacity, 2 * half), 1) == column).astype(jnp.float32).astype(jnp.bfloat16)
        lookup = jnp.dot(hot, table, preferred_element_type=jnp.float32)
        residual = block[0:capacity, :].astype(jnp.float32) - lookup
        amax = jnp.max(jnp.abs(residual), axis=1, keepdims=True)
        source = me ^ k
        codes[pl.ds(pl.multiple_of(source * capacity, capacity), capacity), :] = (
            residual * (127.0 / (amax + 1e-06))
        ).astype(jnp.bfloat16)
        scales[pl.ds(source, 1), :] = jnp.sum(
            jnp.where(eye, amax / 127.0, 0.0), axis=0, keepdims=True
        )


def _call(kernel, outs, args, flops=0):
    moved = sum(a.size * a.dtype.itemsize for a in args) + sum(
        o.size * o.dtype.itemsize for o in outs
    )
    return pl.pallas_call(
        kernel,
        out_shape=outs,
        in_specs=[SMEM if a.ndim == 1 else VMEM for a in args],
        out_specs=[VMEM] * len(outs),
        compiler_params=pltpu.CompilerParams(vmem_limit_bytes=24 * 2**20),
        cost_estimate=pl.CostEstimate(flops=flops, bytes_accessed=moved, transcendentals=0),
    )(*args)


def per_device_eight(embeds, assign, list_slot, old_centroids):
    list_dev, width = old_centroids.shape
    item_dev = embeds.shape[0]
    peers = lax.axis_size("items")
    capacity = 4 * item_dev // peers
    half = list_dev // 2
    hop = lambda a, axis, bit: lax.ppermute(
        a, axis, [(i, i ^ bit) for i in range(lax.axis_size(axis))]
    )
    at = jnp.stack([lax.axis_index("items"), lax.axis_index("rep") & 1]).astype(jnp.int32)
    far_rows = hop(embeds, "items", 4)
    far_assign = hop(assign, "items", 4)
    block = jax.ShapeDtypeStruct((capacity + HEAD, width), jnp.bfloat16)
    *own, far = _call(
        lambda *refs: _route_own_kernel(list_dev, *refs),
        [block] * 4 + [jax.ShapeDtypeStruct((8, item_dev), jnp.int32)],
        (
            at,
            assign.reshape(1, item_dev),
            far_assign.reshape(1, item_dev),
            list_slot.reshape(-1, 128),
            embeds,
        ),
        flops=2 * 4 * capacity * item_dev * width,
    )
    own = [own[0]] + [hop(own[k], "items", k) for k in (1, 2, 3)]
    away = _call(
        _route_far_kernel, [block] * 4, (far, far_rows), flops=2 * 4 * capacity * item_dev * width
    )
    away = [away[0]] + [hop(away[k], "items", k) for k in (1, 2, 3)]
    blocks = tuple(own) + tuple(away)
    partial = jax.ShapeDtypeStruct((half + 8, width), jnp.float32)
    send, keep = _call(
        _sums_kernel,
        [partial] * 2,
        (at,) + blocks,
        flops=2 * list_dev * peers * capacity * width,
    )
    part = keep + hop(send, "rep", 1)
    got = hop(part, "rep", 2)
    (mine,) = _call(
        _fresh_kernel,
        [jax.ShapeDtypeStruct((half, width), jnp.bfloat16)],
        (at, part, got, old_centroids),
    )
    other = hop(mine, "rep", 1)
    fresh, codes, scales = _call(
        _codes_kernel,
        [
            jax.ShapeDtypeStruct((list_dev, width), jnp.bfloat16),
            jax.ShapeDtypeStruct((peers * capacity, width), jnp.bfloat16),
            jax.ShapeDtypeStruct((peers, capacity), jnp.float32),
        ],
        (at,) + blocks + (mine, other),
        flops=2 * list_dev * peers * capacity * width,
    )
    return (
        fresh,
        codes.reshape(1, 1, peers * capacity, width),
        scales.reshape(1, 1, peers * capacity),
    )


def per_device(embeds, assign, list_slot, old_centroids):
    peers = lax.axis_size("items")
    list_dev = old_centroids.shape[0]
    width = embeds.shape[1]
    item_dev = embeds.shape[0]
    capacity = 4 * item_dev // peers
    slot = list_slot[assign]
    owner = slot // list_dev
    local = slot % list_dev
    member = (owner[:, None] == jnp.arange(peers, dtype=jnp.int32)[None, :]).astype(jnp.int32)
    rank = jnp.sum(member * (jnp.cumsum(member, axis=0) - 1), axis=1)
    target = owner * capacity + rank
    outgoing = jnp.zeros((peers * capacity, width), jnp.bfloat16).at[target].set(embeds)
    labels = jnp.full((peers * capacity,), -1, jnp.int32).at[target].set(local)
    arrived, arrived_ids = (
        lax.all_to_all(
            outgoing.reshape(peers, capacity, width),
            "items",
            split_axis=0,
            concat_axis=0,
            tiled=True,
        ),
        lax.all_to_all(
            labels.reshape(peers, capacity), "items", split_axis=0, concat_axis=0, tiled=True
        ),
    )
    arrived = arrived.reshape(peers * capacity, width)
    arrived_ids = arrived_ids.reshape(peers * capacity)
    member_t = (jnp.arange(list_dev, dtype=jnp.int32)[:, None] == arrived_ids[None, :]).astype(
        jnp.bfloat16
    )
    partial_sums = jnp.dot(member_t, arrived, preferred_element_type=jnp.float32)
    partial_counts = jnp.sum(member_t, axis=1, dtype=jnp.float32)
    total_sums, total_counts = lax.psum((partial_sums, partial_counts), "rep")
    fresh = (
        (total_sums + old_centroids.astype(jnp.float32)) / (total_counts + 1.0)[:, None]
    ).astype(jnp.bfloat16)
    lookup = lax.dot_general(
        member_t, fresh, (((0,), (0,)), ((), ())), preferred_element_type=jnp.float32
    )
    residual = arrived.astype(jnp.float32) - lookup
    amax = jnp.max(jnp.abs(residual), axis=1)
    codes = (residual * (127.0 / (amax + 1e-06))[:, None]).astype(jnp.bfloat16)
    row_scales = amax / 127.0
    return (
        fresh,
        codes.reshape(1, 1, peers * capacity, width),
        row_scales.reshape(1, 1, peers * capacity),
    )


def solution(mesh):
    in_specs = (P(("items", "rep"), None), P(("items", "rep")), P(), P("items", None))
    out_specs = (P("items", None), P("items", "rep", None, None), P("items", "rep", None))
    small = mesh.shape["items"] == 8 and mesh.shape["rep"] == 4
    return jax.shard_map(
        per_device_eight if small else per_device,
        mesh=mesh,
        in_specs=in_specs,
        out_specs=out_specs,
        check_vma=False,
    )
```

```python
import jax
import jax.numpy as jnp
from jax import lax
from jax.experimental import pallas as pl
from jax.experimental.pallas import tpu as pltpu
from jax.sharding import PartitionSpec as P

HEAD = 16
VMEM = pl.BlockSpec(memory_space=pltpu.VMEM)


def _log2(n):
    return n.bit_length() - 1


def _iota(shape, dim):
    return lax.broadcasted_iota(jnp.int32, shape, dim)


def _bf16(a):
    return a.astype(jnp.float32).astype(jnp.bfloat16)


def _slots(table, assign):
    t, n = table.shape[0], assign.shape[1]
    hot = _bf16(_iota((t, n), 0) == (assign >> 7))
    lane = _iota((128, n), 0) == (assign & 127)

    def pick(part):
        rows = lax.dot_general(
            _bf16(part), hot, (((0,), (0,)), ((), ())), preferred_element_type=jnp.float32
        )
        return jnp.sum(jnp.where(lane, rows, 0.0), axis=0, keepdims=True)

    return (pick(table & 255) + 256.0 * pick(table >> 8)).astype(jnp.int32)


def _head(list_dev, base, table, assign):
    n = assign.shape[1]
    slot = _slots(table, assign)
    relative = (slot >> _log2(list_dev)) ^ base
    code = (slot & (list_dev - 1)) + 1
    member = (_iota((16, n), 0) == relative).astype(jnp.float32)
    before = _bf16(_iota((n, n), 0) < _iota((n, n), 1))
    count = jnp.dot(member.astype(jnp.bfloat16), before, preferred_element_type=jnp.float32)
    head = jnp.where(member > 0.0, count, -1.0).astype(jnp.int32)[0:8, :]
    row = _iota((8, n), 0)
    head = jnp.where(row == 4, code & 255, head)
    return jnp.where(row == 5, code >> 8, head)


def _route(head, rows, outs, half):
    n = rows.shape[0]
    capacity = rows.shape[1] // 2
    base = half * (capacity + HEAD)
    hot = jnp.concatenate(
        [(_iota((capacity, n), 0) == head[k : k + 1, :]).astype(jnp.float32) for k in range(len(outs))],
        axis=0,
    ).astype(jnp.bfloat16)
    moved = jnp.dot(hot, rows, preferred_element_type=jnp.float32).astype(jnp.bfloat16)
    lo, hi = head[4:5, :].astype(jnp.float32), head[5:6, :].astype(jnp.float32)
    values = jnp.where(_iota((HEAD, n), 0) == 0, lo, hi).astype(jnp.bfloat16)
    labels = lax.dot_general(
        values, hot, (((1,), (1,)), ((), ())), preferred_element_type=jnp.float32
    )
    for i, out in enumerate(outs):
        part = labels[:, i * capacity : (i + 1) * capacity]
        line = jnp.concatenate([part[0:1, :], part[1:2, :]], axis=1)
        out[base : base + capacity, :] = moved[i * capacity : (i + 1) * capacity, :]
        out[base + capacity : base + capacity + HEAD, :] = jnp.broadcast_to(
            line, (HEAD, line.shape[1])
        ).astype(jnp.bfloat16)


def _payload_head(list_dev, base, table, payload):
    n = payload.shape[0] - HEAD
    low = payload[n:, :].astype(jnp.float32)
    assign = (low[0:1, :] + 256.0 * low[1:2, :]).astype(jnp.int32)
    return _head(list_dev, base, table[...], assign)


def _pair_kernel(list_dev, mine, side, table, o0, o1, o2, o3):
    n = mine.shape[0] - HEAD
    for half, payload in enumerate((mine, side)):
        head = _payload_head(list_dev, lax.axis_index("items"), table, payload)
        _route(head, payload[0:n, :], (o0, o1, o2, o3), half)


def _labels(head):
    head = head.astype(jnp.float32)[0:1, :]
    capacity = head.shape[1] // 2
    return (head[:, :capacity] + 256.0 * head[:, capacity:]).astype(jnp.int32) - 1


def _parts(block):
    capacity = block.shape[1] // 2
    size = capacity + HEAD
    return [
        (block[i : i + capacity, :], _labels(block[i + capacity : i + size, :]))
        for i in range(0, block.shape[0], size)
    ]


def _totals(blocks, lists):
    rows = jnp.concatenate([r for r, _ in blocks], axis=0)
    labels = jnp.concatenate([l for _, l in blocks], axis=1)
    hot = (_iota((lists, rows.shape[0]), 0) == labels).astype(jnp.float32)
    sums = jnp.dot(hot.astype(jnp.bfloat16), rows, preferred_element_type=jnp.float32)
    return sums, jnp.sum(hot, axis=1, keepdims=True)


def _both_planes(pairs, lists):
    parts = [_parts(p) for p in pairs]
    mine, mine_n = _totals([p[0] for p in parts], lists)
    side, side_n = _totals([p[1] for p in parts], lists)
    width = mine.shape[1]
    eye = _iota((width, width), 0) == _iota((width, width), 1)
    count = mine_n + side_n
    lines = [
        jnp.sum(jnp.where(eye, count[i : i + width, :], 0.0), axis=0, keepdims=True)
        for i in range(0, lists, width)
    ]
    row = _iota((8, width), 0)
    count = jnp.zeros((8, width), jnp.float32)
    for i, line in enumerate(lines):
        count = jnp.where(row == i, line, count)
    return mine + side, count


def _early_kernel(p0, p1, p2, p3, q0, out):
    lists = out.shape[0] - 8
    out[0:lists, :], out[lists:, :] = _both_planes((p0, p1, p2, p3, q0), lists)


def _late_kernel(early, q1, q2, q3, out):
    lists = out.shape[0] - 8
    sums, count = _both_planes((q1, q2, q3), lists)
    out[0:lists, :] = early[0:lists, :] + sums
    out[lists:, :] = early[lists:, :] + count


def _codes_kernel(mine, other, old, *refs):
    (*blocks, fresh, codes, scales) = refs
    lists, width = fresh.shape
    capacity = width // 2
    me = lax.axis_index("items")
    wide = _iota((width, width), 0) == _iota((width, width), 1)
    for i in range(lists // width):
        row = mine[lists + i : lists + i + 1, :] + other[lists + i : lists + i + 1, :]
        counts = jnp.sum(jnp.where(wide, row, 0.0), axis=1, keepdims=True)
        at_i = slice(i * width, (i + 1) * width)
        total = mine[at_i, :] + other[at_i, :] + old[at_i, :].astype(jnp.float32)
        fresh[at_i, :] = (total / (counts + 1.0)).astype(jnp.bfloat16)
    table = fresh[...]
    eye = _iota((capacity, capacity), 0) == _iota((capacity, capacity), 1)
    for k, (rows, labels) in enumerate(_parts(b)[0] for b in blocks):
        column = jnp.sum(
            jnp.where(eye, labels.astype(jnp.float32), 0.0), axis=1, keepdims=True
        ).astype(jnp.int32)
        hot = _bf16(_iota((capacity, lists), 1) == column)
        lookup = jnp.dot(hot, table, preferred_element_type=jnp.float32)
        residual = rows.astype(jnp.float32) - lookup
        amax = jnp.max(jnp.abs(residual), axis=1, keepdims=True)
        source = me ^ k
        codes[pl.ds(pl.multiple_of(source * capacity, capacity), capacity), :] = (
            residual * (127.0 / (amax + 1e-06))
        ).astype(jnp.bfloat16)
        scales[pl.ds(source, 1), :] = jnp.sum(
            jnp.where(eye, amax / 127.0, 0.0), axis=0, keepdims=True
        )


def _call(kernel, outs, args, flops=0, **options):
    moved = sum(a.size * a.dtype.itemsize for a in args) + sum(
        o.size * o.dtype.itemsize for o in outs
    )
    limit = options.pop("limit", 24 * 2**20)
    return pl.pallas_call(
        kernel,
        out_shape=outs,
        in_specs=[VMEM] * len(args),
        out_specs=[VMEM] * len(outs),
        compiler_params=pltpu.CompilerParams(vmem_limit_bytes=limit),
        cost_estimate=pl.CostEstimate(flops=flops, bytes_accessed=moved, transcendentals=0),
        **options,
    )(*args)


def per_device_eight(embeds, assign, list_slot, old_centroids):
    list_dev, width = old_centroids.shape
    item_dev = embeds.shape[0]
    peers, reps = lax.axis_size("items"), lax.axis_size("rep")
    capacity = 4 * item_dev // peers

    def hop(a, items, rep=0):
        swap = items * reps + rep
        return lax.ppermute(a, ("items", "rep"), [(i, i ^ swap) for i in range(peers * reps)])

    table = list_slot.reshape(-1, 128)
    pair = jax.ShapeDtypeStruct((2 * (capacity + HEAD), width), jnp.bfloat16)
    flops = 2 * 8 * capacity * item_dev * width
    row = lax.broadcasted_iota(jnp.int32, (item_dev + HEAD, width), 0)
    ids = jnp.where(row == item_dev, assign & 255, assign >> 8).astype(jnp.bfloat16)
    payload = jnp.where(row < item_dev, jnp.pad(embeds, ((0, HEAD), (0, 0))), ids)
    far = hop(payload, 4)
    side = hop(payload, 0, 2)

    def routed(mine, side):
        return _call(
            lambda *refs: _pair_kernel(list_dev, *refs),
            [pair] * 4,
            (mine, side, table),
            flops=flops,
        )

    def to_owners(pairs):
        return [pairs[0]] + [hop(pairs[k], k) for k in (3, 2, 1)][::-1]

    near = routed(payload, side)
    far, *near = lax.optimization_barrier((far, *near))
    far_side = hop(far, 0, 2)
    near = to_owners(near)
    away = to_owners(routed(far, far_side))
    total = jax.ShapeDtypeStruct((list_dev + 8, width), jnp.float32)
    flops = 2 * list_dev * capacity * width
    (early,) = _call(_early_kernel, [total], (*near, away[0]), flops=10 * flops)
    (mine,) = _call(_late_kernel, [total], (early, *away[1:]), flops=6 * flops)
    other = hop(mine, 0, 1)
    fresh, codes, scales = _call(
        _codes_kernel,
        [
            jax.ShapeDtypeStruct((list_dev, width), jnp.bfloat16),
            jax.ShapeDtypeStruct((peers * capacity, width), jnp.bfloat16),
            jax.ShapeDtypeStruct((peers, capacity), jnp.float32),
        ],
        (mine, other, old_centroids, *near, *away),
        flops=8 * flops,
    )
    return (
        fresh,
        codes.reshape(1, 1, peers * capacity, width),
        scales.reshape(1, 1, peers * capacity),
    )


def per_device(embeds, assign, list_slot, old_centroids):
    peers = lax.axis_size("items")
    list_dev = old_centroids.shape[0]
    width = embeds.shape[1]
    item_dev = embeds.shape[0]
    capacity = 4 * item_dev // peers
    slot = list_slot[assign]
    owner = slot // list_dev
    local = slot % list_dev
    member = (owner[:, None] == jnp.arange(peers, dtype=jnp.int32)[None, :]).astype(jnp.int32)
    rank = jnp.sum(member * (jnp.cumsum(member, axis=0) - 1), axis=1)
    target = owner * capacity + rank
    outgoing = jnp.zeros((peers * capacity, width), jnp.bfloat16).at[target].set(embeds)
    labels = jnp.full((peers * capacity,), -1, jnp.int32).at[target].set(local)
    arrived, arrived_ids = (
        lax.all_to_all(
            outgoing.reshape(peers, capacity, width),
            "items",
            split_axis=0,
            concat_axis=0,
            tiled=True,
        ),
        lax.all_to_all(
            labels.reshape(peers, capacity), "items", split_axis=0, concat_axis=0, tiled=True
        ),
    )
    arrived = arrived.reshape(peers * capacity, width)
    arrived_ids = arrived_ids.reshape(peers * capacity)
    member_t = (jnp.arange(list_dev, dtype=jnp.int32)[:, None] == arrived_ids[None, :]).astype(
        jnp.bfloat16
    )
    partial_sums = jnp.dot(member_t, arrived, preferred_element_type=jnp.float32)
    partial_counts = jnp.sum(member_t, axis=1, dtype=jnp.float32)
    total_sums, total_counts = lax.psum((partial_sums, partial_counts), "rep")
    fresh = (
        (total_sums + old_centroids.astype(jnp.float32)) / (total_counts + 1.0)[:, None]
    ).astype(jnp.bfloat16)
    lookup = lax.dot_general(
        member_t, fresh, (((0,), (0,)), ((), ())), preferred_element_type=jnp.float32
    )
    residual = arrived.astype(jnp.float32) - lookup
    amax = jnp.max(jnp.abs(residual), axis=1)
    codes = (residual * (127.0 / (amax + 1e-06))[:, None]).astype(jnp.bfloat16)
    row_scales = amax / 127.0
    return (
        fresh,
        codes.reshape(1, 1, peers * capacity, width),
        row_scales.reshape(1, 1, peers * capacity),
    )


def solution(mesh):
    in_specs = (P(("items", "rep"), None), P(("items", "rep")), P(), P("items", None))
    out_specs = (P("items", None), P("items", "rep", None, None), P("items", "rep", None))
    small = mesh.shape["items"] == 8 and mesh.shape["rep"] == 4
    return jax.shard_map(
        per_device_eight if small else per_device,
        mesh=mesh,
        in_specs=in_specs,
        out_specs=out_specs,
        check_vma=False,
    )
```

```python
import jax
import jax.numpy as jnp
from jax import lax
from jax.experimental import pallas as pl
from jax.experimental.pallas import tpu as pltpu
from jax.sharding import PartitionSpec as P

HEAD = 16
VMEM = pl.BlockSpec(memory_space=pltpu.VMEM)


def _log2(n):
    return n.bit_length() - 1


def _iota(shape, dim):
    return lax.broadcasted_iota(jnp.int32, shape, dim)


def _bf16(a):
    return a.astype(jnp.float32).astype(jnp.bfloat16)


def _slots(table, assign):
    t, n = table.shape[0], assign.shape[1]
    hot = _bf16(_iota((t, n), 0) == (assign >> 7))
    lane = _iota((128, n), 0) == (assign & 127)

    def pick(part):
        rows = lax.dot_general(
            _bf16(part), hot, (((0,), (0,)), ((), ())), preferred_element_type=jnp.float32
        )
        return jnp.sum(jnp.where(lane, rows, 0.0), axis=0, keepdims=True)

    return (pick(table & 255) + 256.0 * pick(table >> 8)).astype(jnp.int32)


def _core():
    return lax.axis_index("rep") & 1


def _head(list_dev, me, table, payload):
    n = payload.shape[0] - HEAD
    low = payload[n:, :].astype(jnp.float32)
    slot = _slots(table, (low[0:1, :] + 256.0 * low[1:2, :]).astype(jnp.int32))
    relative = (slot >> _log2(list_dev)) ^ me
    code = (slot & (list_dev - 1)) + 1
    member = (_iota((HEAD, n), 0) == relative).astype(jnp.float32)
    before = _bf16(_iota((n, n), 0) < _iota((n, n), 1))
    count = jnp.dot(member.astype(jnp.bfloat16), before, preferred_element_type=jnp.float32)
    rank = jnp.sum(member * count, axis=0, keepdims=True).astype(jnp.int32)
    return rank, relative, (code & 255).astype(jnp.float32), (code >> 8).astype(jnp.float32)


def _route(head, rows, outs, base):
    rank, relative, lo, hi = head
    n = rows.shape[0]
    capacity = n // 2
    hot = jnp.concatenate(
        [
            (_iota((capacity, n), 0) == jnp.where(relative == k, rank, -1)).astype(jnp.float32)
            for k, _ in outs
        ],
        axis=0,
    ).astype(jnp.bfloat16)
    moved = jnp.dot(hot, rows, preferred_element_type=jnp.float32).astype(jnp.bfloat16)
    values = jnp.where(_iota((HEAD, n), 0) == 0, lo, hi).astype(jnp.bfloat16)
    labels = lax.dot_general(
        values, hot, (((1,), (1,)), ((), ())), preferred_element_type=jnp.float32
    )
    for i, (_, out) in enumerate(outs):
        at = slice(i * capacity, (i + 1) * capacity)
        line = jnp.concatenate([labels[0:1, at], labels[1:2, at]], axis=1)
        out[base : base + capacity, :] = moved[at, :]
        out[base + capacity : base + capacity + HEAD, :] = jnp.broadcast_to(
            line, (HEAD, line.shape[1])
        ).astype(jnp.bfloat16)


def _split_kernel(list_dev, payload, twin, table, *refs):
    a, b = refs[-2:]
    core, me = _core(), lax.axis_index("items")
    n = payload.shape[0] - HEAD
    size = n // 2 + HEAD
    mine, other = payload[...], twin[...]
    for i in range(2):
        part = jnp.where(core == i, mine, other)
        head = _head(list_dev, me, table[...], part)
        _route(head, part[0:n, :], ((1 + 2 * core, a), (2 - 2 * core, b)), i * size)


def _labels(head):
    head = head.astype(jnp.float32)[0:1, :]
    capacity = head.shape[1] // 2
    return (head[:, :capacity] + 256.0 * head[:, capacity:]).astype(jnp.int32) - 1


def _parts(block):
    capacity = block.shape[1] // 2
    size = capacity + HEAD
    return [
        (block[i : i + capacity, :], _labels(block[i + capacity : i + size, :]))
        for i in range(0, block.shape[0], size)
    ]


def _totals(blocks, lists):
    parts = [p for b in blocks for p in _parts(b)]
    rows = jnp.concatenate([r for r, _ in parts], axis=0)
    labels = jnp.concatenate([l for _, l in parts], axis=1)
    hot = (_iota((lists, rows.shape[0]), 0) == labels).astype(jnp.float32)
    sums = jnp.dot(hot.astype(jnp.bfloat16), rows, preferred_element_type=jnp.float32)
    return sums, jnp.sum(hot, axis=1, keepdims=True)


def _sums_kernel(*refs):
    *before, a, b, side_a, side_b, out, pack = refs
    lists, width = out.shape[0] - 8, out.shape[1]
    mine, mine_n = _totals((a, b), lists)
    side, side_n = _totals((side_a, side_b), lists)
    count = mine_n + side_n
    eye = _iota((width, width), 0) == _iota((width, width), 1)
    row = _iota((8, width), 0)
    lines = jnp.zeros((8, width), jnp.float32)
    for i in range(lists // width):
        line = jnp.where(eye, count[i * width : (i + 1) * width, :], 0.0)
        lines = jnp.where(row == i, jnp.sum(line, axis=0, keepdims=True), lines)
    if before:
        out[0:lists, :] = before[0][0:lists, :] + (mine + side)
        out[lists:, :] = before[0][lists:, :] + lines
    else:
        out[0:lists, :] = mine + side
        out[lists:, :] = lines
    size = a.shape[0] // 2
    for i, block in enumerate((a, b)):
        pack[i * size : (i + 1) * size, :] = jnp.where(
            _core() == 0, block[size:, :], block[0:size, :]
        )


def _codes_kernel(mine, other, old, *refs):
    (*blocks, fresh, codes, scales) = refs
    lists, width = fresh.shape
    capacity = width // 2
    me, core = lax.axis_index("items"), _core()
    wide = _iota((width, width), 0) == _iota((width, width), 1)
    for i in range(lists // width):
        row = mine[lists + i : lists + i + 1, :] + other[lists + i : lists + i + 1, :]
        counts = jnp.sum(jnp.where(wide, row, 0.0), axis=1, keepdims=True)
        at_i = slice(i * width, (i + 1) * width)
        total = mine[at_i, :] + other[at_i, :] + old[at_i, :].astype(jnp.float32)
        fresh[at_i, :] = (total / (counts + 1.0)).astype(jnp.bfloat16)
    table = fresh[...]
    eye = _iota((capacity, capacity), 0) == _iota((capacity, capacity), 1)
    size = capacity + HEAD
    ordered = []
    for i, (a, b, pack) in enumerate((blocks[0:3], blocks[3:6])):
        base = me ^ (4 * i)
        for block, k in ((a, 1 + 2 * core), (b, 2 - 2 * core)):
            part = jnp.where(core == 0, block[0:size, :], block[size:, :])
            ordered.append((base ^ k, _parts(part)[0]))
        for part, k in zip(_parts(pack), (3 - 2 * core, 2 * core)):
            ordered.append((base ^ k, part))
    for source, (rows, labels) in ordered:
        column = jnp.sum(
            jnp.where(eye, labels.astype(jnp.float32), 0.0), axis=1, keepdims=True
        ).astype(jnp.int32)
        hot = _bf16(_iota((capacity, lists), 1) == column)
        lookup = jnp.dot(hot, table, preferred_element_type=jnp.float32)
        residual = rows.astype(jnp.float32) - lookup
        amax = jnp.max(jnp.abs(residual), axis=1, keepdims=True)
        codes[pl.ds(pl.multiple_of(source * capacity, capacity), capacity), :] = (
            residual * (127.0 / (amax + 1e-06))
        ).astype(jnp.bfloat16)
        scales[pl.ds(source, 1), :] = jnp.sum(
            jnp.where(eye, amax / 127.0, 0.0), axis=0, keepdims=True
        )


def _call(kernel, outs, args, flops=0, **options):
    moved = sum(a.size * a.dtype.itemsize for a in args) + sum(
        o.size * o.dtype.itemsize for o in outs
    )
    limit = options.pop("limit", 24 * 2**20)
    return pl.pallas_call(
        kernel,
        out_shape=outs,
        in_specs=[VMEM] * len(args),
        out_specs=[VMEM] * len(outs),
        compiler_params=pltpu.CompilerParams(vmem_limit_bytes=limit),
        cost_estimate=pl.CostEstimate(flops=flops, bytes_accessed=moved, transcendentals=0),
        **options,
    )(*args)


def per_device_eight(embeds, assign, list_slot, old_centroids):
    list_dev, width = old_centroids.shape
    item_dev = embeds.shape[0]
    peers, reps = lax.axis_size("items"), lax.axis_size("rep")
    capacity = 4 * item_dev // peers

    def hop(a, items, rep=0):
        swap = items * reps + rep
        return lax.ppermute(a, ("items", "rep"), [(i, i ^ swap) for i in range(peers * reps)])

    table = list_slot.reshape(-1, 128)
    pair = jax.ShapeDtypeStruct((2 * (capacity + HEAD), width), jnp.bfloat16)
    total = jax.ShapeDtypeStruct((list_dev + 8, width), jnp.float32)
    flops = 2 * 4 * capacity * item_dev * width

    def spread(a, items, rep):
        swap = [x * reps + rep for x in items]
        return lax.ppermute(a, ("items", "rep"), [(i, i ^ swap[i & 1]) for i in range(peers * reps)])

    def to_owners(payload, weight, *after):
        a, b = _call(
            lambda *refs: _split_kernel(list_dev, *refs),
            [pair] * 2,
            (payload, hop(payload, 0, 1), table, *after),
            flops=weight * flops,
        )
        side_b, near_b = spread(b, (2, 0), 2), spread(b, (2, 0), 0)
        side_a, near_a = spread(a, (1, 3), 2), spread(a, (1, 3), 0)
        return near_a, near_b, side_a, side_b

    row = lax.broadcasted_iota(jnp.int32, (item_dev + HEAD, width), 0)
    ids = jnp.where(row == item_dev, assign & 255, assign >> 8).astype(jnp.bfloat16)
    payload = jnp.where(row < item_dev, jnp.pad(embeds, ((0, HEAD), (0, 0))), ids)
    far = hop(payload, 4)
    near = to_owners(payload, 1000)
    away = to_owners(far, 1, near[3])
    flops = 2 * list_dev * capacity * width
    mine, near_pack = _call(_sums_kernel, [total, pair], near, flops=8 * flops)
    near_pack = hop(near_pack, 0, 1)
    mine, away_pack = _call(_sums_kernel, [total, pair], (mine, *away), flops=8 * flops)
    away_pack = hop(away_pack, 0, 1)
    other = hop(mine, 0, 1)
    fresh, codes, scales = _call(
        _codes_kernel,
        [
            jax.ShapeDtypeStruct((list_dev, width), jnp.bfloat16),
            jax.ShapeDtypeStruct((peers * capacity, width), jnp.bfloat16),
            jax.ShapeDtypeStruct((peers, capacity), jnp.float32),
        ],
        (mine, other, old_centroids, *near[0:2], near_pack, *away[0:2], away_pack),
        flops=8 * flops,
    )
    return (
        fresh,
        codes.reshape(1, 1, peers * capacity, width),
        scales.reshape(1, 1, peers * capacity),
    )


def per_device(embeds, assign, list_slot, old_centroids):
    peers = lax.axis_size("items")
    list_dev = old_centroids.shape[0]
    width = embeds.shape[1]
    item_dev = embeds.shape[0]
    capacity = 4 * item_dev // peers
    slot = list_slot[assign]
    owner = slot // list_dev
    local = slot % list_dev
    member = (owner[:, None] == jnp.arange(peers, dtype=jnp.int32)[None, :]).astype(jnp.int32)
    rank = jnp.sum(member * (jnp.cumsum(member, axis=0) - 1), axis=1)
    target = owner * capacity + rank
    outgoing = jnp.zeros((peers * capacity, width), jnp.bfloat16).at[target].set(embeds)
    labels = jnp.full((peers * capacity,), -1, jnp.int32).at[target].set(local)
    arrived, arrived_ids = (
        lax.all_to_all(
            outgoing.reshape(peers, capacity, width),
            "items",
            split_axis=0,
            concat_axis=0,
            tiled=True,
        ),
        lax.all_to_all(
            labels.reshape(peers, capacity), "items", split_axis=0, concat_axis=0, tiled=True
        ),
    )
    arrived = arrived.reshape(peers * capacity, width)
    arrived_ids = arrived_ids.reshape(peers * capacity)
    member_t = (jnp.arange(list_dev, dtype=jnp.int32)[:, None] == arrived_ids[None, :]).astype(
        jnp.bfloat16
    )
    partial_sums = jnp.dot(member_t, arrived, preferred_element_type=jnp.float32)
    partial_counts = jnp.sum(member_t, axis=1, dtype=jnp.float32)
    total_sums, total_counts = lax.psum((partial_sums, partial_counts), "rep")
    fresh = (
        (total_sums + old_centroids.astype(jnp.float32)) / (total_counts + 1.0)[:, None]
    ).astype(jnp.bfloat16)
    lookup = lax.dot_general(
        member_t, fresh, (((0,), (0,)), ((), ())), preferred_element_type=jnp.float32
    )
    residual = arrived.astype(jnp.float32) - lookup
    amax = jnp.max(jnp.abs(residual), axis=1)
    codes = (residual * (127.0 / (amax + 1e-06))[:, None]).astype(jnp.bfloat16)
    row_scales = amax / 127.0
    return (
        fresh,
        codes.reshape(1, 1, peers * capacity, width),
        row_scales.reshape(1, 1, peers * capacity),
    )


def solution(mesh):
    in_specs = (P(("items", "rep"), None), P(("items", "rep")), P(), P("items", None))
    out_specs = (P("items", None), P("items", "rep", None, None), P("items", "rep", None))
    small = mesh.shape["items"] == 8 and mesh.shape["rep"] == 4
    return jax.shard_map(
        per_device_eight if small else per_device,
        mesh=mesh,
        in_specs=in_specs,
        out_specs=out_specs,
        check_vma=False,
    )
```

```python
import jax
import jax.numpy as jnp
from jax import lax
from jax.experimental import pallas as pl
from jax.experimental.pallas import tpu as pltpu
from jax.sharding import PartitionSpec as P

HEAD = 16
VMEM = pl.BlockSpec(memory_space=pltpu.VMEM)


def _log2(n):
    return n.bit_length() - 1


def _iota(shape, dim):
    return lax.broadcasted_iota(jnp.int32, shape, dim)


def _bf16(a):
    return a.astype(jnp.float32).astype(jnp.bfloat16)


def _slots(table, assign):
    t, n = table.shape[0], assign.shape[1]
    hot = _bf16(_iota((t, n), 0) == (assign >> 7))
    lane = _iota((128, n), 0) == (assign & 127)

    def pick(part):
        rows = lax.dot_general(
            _bf16(part), hot, (((0,), (0,)), ((), ())), preferred_element_type=jnp.float32
        )
        return jnp.sum(jnp.where(lane, rows, 0.0), axis=0, keepdims=True)

    return (pick(table & 255) + 256.0 * pick(table >> 8)).astype(jnp.int32)


def _core():
    return lax.axis_index("rep") & 1


def _heads(list_dev, me, table, payloads):
    n = payloads[0].shape[0] - HEAD
    low = jnp.concatenate([p[n:, :].astype(jnp.float32) for p in payloads], axis=1)
    slot = _slots(table, (low[0:1, :] + 256.0 * low[1:2, :]).astype(jnp.int32))
    relative = (slot >> _log2(list_dev)) ^ me
    code = (slot & (list_dev - 1)) + 1
    lo, hi = (code & 255).astype(jnp.float32), (code >> 8).astype(jnp.float32)
    member = (_iota((HEAD, low.shape[1]), 0) == relative).astype(jnp.float32)
    at = [slice(i * n, (i + 1) * n) for i in range(len(payloads))]
    before = _bf16(_iota((n, n), 0) < _iota((n, n), 1))
    count = jnp.dot(
        jnp.concatenate([member[:, i] for i in at], axis=0).astype(jnp.bfloat16),
        before,
        preferred_element_type=jnp.float32,
    )
    out = []
    for j, i in enumerate(at):
        rank = jnp.sum(member[:, i] * count[j * HEAD : (j + 1) * HEAD, :], axis=0, keepdims=True)
        out.append((rank.astype(jnp.int32), relative[:, i], lo[:, i], hi[:, i]))
    return out


def _route(head, rows, ks):
    rank, relative, lo, hi = head
    n = rows.shape[0]
    capacity = n // 2
    hot = jnp.concatenate(
        [
            (_iota((capacity, n), 0) == jnp.where(relative == k, rank, -1)).astype(jnp.float32)
            for k in ks
        ],
        axis=0,
    ).astype(jnp.bfloat16)
    moved = jnp.dot(hot, rows, preferred_element_type=jnp.float32).astype(jnp.bfloat16)
    values = jnp.where(_iota((HEAD, n), 0) == 0, lo, hi).astype(jnp.bfloat16)
    labels = lax.dot_general(
        values, hot, (((1,), (1,)), ((), ())), preferred_element_type=jnp.float32
    )
    at = [slice(i * capacity, (i + 1) * capacity) for i in range(len(ks))]
    return [
        (moved[i, :], jnp.concatenate([labels[0:1, i], labels[1:2, i]], axis=1)) for i in at
    ]


def _owners():
    return 1 - _core(), 2 + _core()


def _split_kernel(list_dev, payload, twin, table, *refs):
    mine, other = payload[...], twin[...]
    both = jnp.where(_core() == 0, mine, other), jnp.where(_core() == 0, other, mine)
    n = mine.shape[0] - HEAD
    heads = _heads(list_dev, lax.axis_index("items"), table[...], both)
    first, second = (_route(h, p[0:n, :], _owners()) for h, p in zip(heads, both))
    for out, (rows0, line0), (rows1, line1) in zip(refs[-2:], first, second):
        capacity = rows0.shape[0]
        out[0:capacity, :] = rows0
        out[capacity : 2 * capacity, :] = rows1
        out[2 * capacity : 2 * capacity + HEAD, :] = jnp.where(
            _iota((HEAD, line0.shape[1]), 0) == 0, line0, line1
        ).astype(jnp.bfloat16)


def _labels(line):
    line = line.astype(jnp.float32)
    capacity = line.shape[1] // 2
    return (line[:, :capacity] + 256.0 * line[:, capacity:]).astype(jnp.int32) - 1


def _parts(block):
    capacity = block.shape[1] // 2
    head = block[2 * capacity :, :].astype(jnp.float32)
    return [
        (block[i * capacity : (i + 1) * capacity, :], _labels(head[i : i + 1, :]))
        for i in range(2)
    ]


def _totals(blocks, lists):
    parts = [p for b in blocks for p in _parts(b)]
    rows = jnp.concatenate([r for r, _ in parts], axis=0)
    labels = jnp.concatenate([l for _, l in parts], axis=1)
    hot = (_iota((lists, rows.shape[0]), 0) == labels).astype(jnp.float32)
    sums = jnp.dot(hot.astype(jnp.bfloat16), rows, preferred_element_type=jnp.float32)
    return sums, jnp.sum(hot, axis=1, keepdims=True)


def _sums_kernel(*refs):
    *before, a, b, side_a, side_b, out, pack = refs
    lists, width = out.shape[0] - 8, out.shape[1]
    mine, mine_n = _totals((a, b), lists)
    side, side_n = _totals((side_a, side_b), lists)
    count = mine_n + side_n
    eye = _iota((width, width), 0) == _iota((width, width), 1)
    row = _iota((8, width), 0)
    lines = jnp.zeros((8, width), jnp.float32)
    for i in range(lists // width):
        line = jnp.where(eye, count[i * width : (i + 1) * width, :], 0.0)
        lines = jnp.where(row == i, jnp.sum(line, axis=0, keepdims=True), lines)
    if before:
        out[0:lists, :] = before[0][0:lists, :] + (mine + side)
        out[lists:, :] = before[0][lists:, :] + lines
    else:
        out[0:lists, :] = mine + side
        out[lists:, :] = lines
    capacity = width // 2
    lines = []
    for i, block in enumerate((a, b)):
        rows = jnp.where(_core() == 0, block[capacity : 2 * capacity, :], block[0:capacity, :])
        pack[i * capacity : (i + 1) * capacity, :] = rows
        head = block[2 * capacity :, :].astype(jnp.float32)
        lines.append(jnp.where(_core() == 0, head[1:2, :], head[0:1, :]))
    pack[2 * capacity :, :] = jnp.where(
        _iota((HEAD, width), 0) == 0, lines[0], lines[1]
    ).astype(jnp.bfloat16)


def _codes_kernel(mine, other, old, *refs):
    (*blocks, fresh, codes, scales) = refs
    lists, width = fresh.shape
    capacity = width // 2
    me, core = lax.axis_index("items"), _core()
    wide = _iota((width, width), 0) == _iota((width, width), 1)
    for i in range(lists // width):
        row = mine[lists + i : lists + i + 1, :] + other[lists + i : lists + i + 1, :]
        counts = jnp.sum(jnp.where(wide, row, 0.0), axis=1, keepdims=True)
        at_i = slice(i * width, (i + 1) * width)
        total = mine[at_i, :] + other[at_i, :] + old[at_i, :].astype(jnp.float32)
        fresh[at_i, :] = (total / (counts + 1.0)).astype(jnp.bfloat16)
    table = fresh[...]
    eye = _iota((capacity, capacity), 0) == _iota((capacity, capacity), 1)
    ordered = []
    for i, (a, b, pack) in enumerate((blocks[0:3], blocks[3:6])):
        base = me ^ (4 * i)
        for block, k in zip((a, b), _owners()):
            (rows0, labels0), (rows1, labels1) = _parts(block)
            part = jnp.where(core == 0, rows0, rows1), jnp.where(core == 0, labels0, labels1)
            ordered.append((base ^ k, part))
        for part, k in zip(_parts(pack), (core, 3 - core)):
            ordered.append((base ^ k, part))
    for source, (rows, labels) in ordered:
        column = jnp.sum(
            jnp.where(eye, labels.astype(jnp.float32), 0.0), axis=1, keepdims=True
        ).astype(jnp.int32)
        hot = _bf16(_iota((capacity, lists), 1) == column)
        lookup = jnp.dot(hot, table, preferred_element_type=jnp.float32)
        residual = rows.astype(jnp.float32) - lookup
        amax = jnp.max(jnp.abs(residual), axis=1, keepdims=True)
        codes[pl.ds(pl.multiple_of(source * capacity, capacity), capacity), :] = (
            residual * (127.0 / (amax + 1e-06))
        ).astype(jnp.bfloat16)
        scales[pl.ds(source, 1), :] = jnp.sum(
            jnp.where(eye, amax / 127.0, 0.0), axis=0, keepdims=True
        )


def _call(kernel, outs, args, flops=0, **options):
    moved = sum(a.size * a.dtype.itemsize for a in args) + sum(
        o.size * o.dtype.itemsize for o in outs
    )
    limit = options.pop("limit", 24 * 2**20)
    return pl.pallas_call(
        kernel,
        out_shape=outs,
        in_specs=[VMEM] * len(args),
        out_specs=[VMEM] * len(outs),
        compiler_params=pltpu.CompilerParams(vmem_limit_bytes=limit),
        cost_estimate=pl.CostEstimate(flops=flops, bytes_accessed=moved, transcendentals=0),
        **options,
    )(*args)


def per_device_eight(embeds, assign, list_slot, old_centroids):
    list_dev, width = old_centroids.shape
    item_dev = embeds.shape[0]
    peers, reps = lax.axis_size("items"), lax.axis_size("rep")
    capacity = 4 * item_dev // peers

    def hop(a, items, rep=0):
        swap = items * reps + rep
        return lax.ppermute(a, ("items", "rep"), [(i, i ^ swap) for i in range(peers * reps)])

    table = list_slot.reshape(-1, 128)
    pair = jax.ShapeDtypeStruct((2 * capacity + HEAD, width), jnp.bfloat16)
    total = jax.ShapeDtypeStruct((list_dev + 8, width), jnp.float32)
    flops = 2 * 4 * capacity * item_dev * width

    def spread(a, items, rep):
        swap = [x * reps + rep for x in items]
        return lax.ppermute(a, ("items", "rep"), [(i, i ^ swap[i & 1]) for i in range(peers * reps)])

    def to_owners(payload, weight, extra, *after):
        wide = jax.ShapeDtypeStruct((pair.shape[0] + extra, width), jnp.bfloat16)
        a, b = _call(
            lambda *refs: _split_kernel(list_dev, *refs),
            [wide] * 2,
            (payload, hop(payload, 0, 1), table, *after),
            flops=weight * flops,
        )
        side_b, near_b = spread(b, (2, 3), 2), spread(b, (2, 3), 0)
        side_a, near_a = spread(a, (1, 0), 2), spread(a, (1, 0), 0)
        return near_a, near_b, side_a, side_b

    row = lax.broadcasted_iota(jnp.int32, (item_dev + HEAD, width), 0)
    ids = jnp.where(row == item_dev, assign & 255, assign >> 8).astype(jnp.bfloat16)
    payload = jnp.where(row < item_dev, jnp.pad(embeds, ((0, HEAD), (0, 0))), ids)
    far = hop(payload, 4)
    near = to_owners(payload, 1000, HEAD)
    away = to_owners(far, 1, 0, *(near[i] for i in (2,)))
    flops = 2 * list_dev * capacity * width
    mine, near_pack = _call(_sums_kernel, [total, pair], near, flops=8 * flops)
    near_pack = hop(near_pack, 0, 1)
    mine, away_pack = _call(_sums_kernel, [total, pair], (mine, *away), flops=8 * flops)
    away_pack = hop(away_pack, 0, 1)
    other = hop(mine, 0, 1)
    fresh, codes, scales = _call(
        _codes_kernel,
        [
            jax.ShapeDtypeStruct((list_dev, width), jnp.bfloat16),
            jax.ShapeDtypeStruct((peers * capacity, width), jnp.bfloat16),
            jax.ShapeDtypeStruct((peers, capacity), jnp.float32),
        ],
        (mine, other, old_centroids, *near[0:2], near_pack, *away[0:2], away_pack),
        flops=8 * flops,
    )
    return (
        fresh,
        codes.reshape(1, 1, peers * capacity, width),
        scales.reshape(1, 1, peers * capacity),
    )


def per_device(embeds, assign, list_slot, old_centroids):
    peers = lax.axis_size("items")
    list_dev = old_centroids.shape[0]
    width = embeds.shape[1]
    item_dev = embeds.shape[0]
    capacity = 4 * item_dev // peers
    slot = list_slot[assign]
    owner = slot // list_dev
    local = slot % list_dev
    member = (owner[:, None] == jnp.arange(peers, dtype=jnp.int32)[None, :]).astype(jnp.int32)
    rank = jnp.sum(member * (jnp.cumsum(member, axis=0) - 1), axis=1)
    target = owner * capacity + rank
    outgoing = jnp.zeros((peers * capacity, width), jnp.bfloat16).at[target].set(embeds)
    labels = jnp.full((peers * capacity,), -1, jnp.int32).at[target].set(local)
    arrived, arrived_ids = (
        lax.all_to_all(
            outgoing.reshape(peers, capacity, width),
            "items",
            split_axis=0,
            concat_axis=0,
            tiled=True,
        ),
        lax.all_to_all(
            labels.reshape(peers, capacity), "items", split_axis=0, concat_axis=0, tiled=True
        ),
    )
    arrived = arrived.reshape(peers * capacity, width)
    arrived_ids = arrived_ids.reshape(peers * capacity)
    member_t = (jnp.arange(list_dev, dtype=jnp.int32)[:, None] == arrived_ids[None, :]).astype(
        jnp.bfloat16
    )
    partial_sums = jnp.dot(member_t, arrived, preferred_element_type=jnp.float32)
    partial_counts = jnp.sum(member_t, axis=1, dtype=jnp.float32)
    total_sums, total_counts = lax.psum((partial_sums, partial_counts), "rep")
    fresh = (
        (total_sums + old_centroids.astype(jnp.float32)) / (total_counts + 1.0)[:, None]
    ).astype(jnp.bfloat16)
    lookup = lax.dot_general(
        member_t, fresh, (((0,), (0,)), ((), ())), preferred_element_type=jnp.float32
    )
    residual = arrived.astype(jnp.float32) - lookup
    amax = jnp.max(jnp.abs(residual), axis=1)
    codes = (residual * (127.0 / (amax + 1e-06))[:, None]).astype(jnp.bfloat16)
    row_scales = amax / 127.0
    return (
        fresh,
        codes.reshape(1, 1, peers * capacity, width),
        row_scales.reshape(1, 1, peers * capacity),
    )


def solution(mesh):
    in_specs = (P(("items", "rep"), None), P(("items", "rep")), P(), P("items", None))
    out_specs = (P("items", None), P("items", "rep", None, None), P("items", "rep", None))
    small = mesh.shape["items"] == 8 and mesh.shape["rep"] == 4
    return jax.shard_map(
        per_device_eight if small else per_device,
        mesh=mesh,
        in_specs=in_specs,
        out_specs=out_specs,
        check_vma=False,
    )
```

```python
import jax
import jax.numpy as jnp
from jax import lax
from jax.experimental import pallas as pl
from jax.experimental.pallas import tpu as pltpu
from jax.sharding import PartitionSpec as P

HEAD = 16
VMEM = pl.BlockSpec(memory_space=pltpu.VMEM)


def _log2(n):
    return n.bit_length() - 1


def _iota(shape, dim):
    return lax.broadcasted_iota(jnp.int32, shape, dim)


def _bf16(a):
    return a.astype(jnp.float32).astype(jnp.bfloat16)


def _slots(table, assign):
    t, n = table.shape[0], assign.shape[1]
    hot = _bf16(_iota((t, n), 0) == (assign >> 7))
    lane = _iota((128, n), 0) == (assign & 127)

    def pick(part):
        rows = lax.dot_general(
            _bf16(part), hot, (((0,), (0,)), ((), ())), preferred_element_type=jnp.float32
        )
        return jnp.sum(jnp.where(lane, rows, 0.0), axis=0, keepdims=True)

    return (pick(table & 255) + 256.0 * pick(table >> 8)).astype(jnp.int32)


def _core():
    return lax.axis_index("rep") & 1


def _heads(list_dev, me, table, payloads):
    n = payloads[0].shape[0] - HEAD
    low = jnp.concatenate([p[n:, :].astype(jnp.float32) for p in payloads], axis=1)
    slot = _slots(table, (low[0:1, :] + 256.0 * low[1:2, :]).astype(jnp.int32))
    relative = (slot >> _log2(list_dev)) ^ me
    code = (slot & (list_dev - 1)) + 1
    lo, hi = (code & 255).astype(jnp.float32), (code >> 8).astype(jnp.float32)
    member = (_iota((HEAD, low.shape[1]), 0) == relative).astype(jnp.float32)
    at = [slice(i * n, (i + 1) * n) for i in range(len(payloads))]
    before = _bf16(_iota((n, n), 0) < _iota((n, n), 1))
    count = jnp.dot(
        jnp.concatenate([member[:, i] for i in at], axis=0).astype(jnp.bfloat16),
        before,
        preferred_element_type=jnp.float32,
    )
    out = []
    for j, i in enumerate(at):
        rank = jnp.sum(member[:, i] * count[j * HEAD : (j + 1) * HEAD, :], axis=0, keepdims=True)
        out.append((rank.astype(jnp.int32), relative[:, i], lo[:, i], hi[:, i]))
    return out


def _route(head, rows, ks):
    rank, relative, lo, hi = head
    n = rows.shape[0]
    capacity = n // 2
    hot = jnp.concatenate(
        [
            (_iota((capacity, n), 0) == jnp.where(relative == k, rank, -1)).astype(jnp.float32)
            for k in ks
        ],
        axis=0,
    ).astype(jnp.bfloat16)
    moved = jnp.dot(hot, rows, preferred_element_type=jnp.float32).astype(jnp.bfloat16)
    values = jnp.where(_iota((HEAD, n), 0) == 0, lo, hi).astype(jnp.bfloat16)
    labels = lax.dot_general(
        values, hot, (((1,), (1,)), ((), ())), preferred_element_type=jnp.float32
    )
    at = [slice(i * capacity, (i + 1) * capacity) for i in range(len(ks))]
    return [
        (moved[i, :], jnp.concatenate([labels[0:1, i], labels[1:2, i]], axis=1)) for i in at
    ]


def _ids_kernel(assign, _, out):
    lo, hi = (assign[...] & 255).astype(jnp.float32), (assign[...] >> 8).astype(jnp.float32)
    n = assign.shape[1]
    out[n:, :] = jnp.where(_iota((HEAD, n), 0) == 0, lo, hi).astype(jnp.bfloat16)


def _owners():
    return 1 - _core(), 2 + _core()


def _split_kernel(list_dev, payload, twin, table, *refs):
    mine, other = payload[...], twin[...]
    both = jnp.where(_core() == 0, mine, other), jnp.where(_core() == 0, other, mine)
    n = mine.shape[0] - HEAD
    heads = _heads(list_dev, lax.axis_index("items"), table[...], both)
    first, second = (_route(h, p[0:n, :], _owners()) for h, p in zip(heads, both))
    for out, (rows0, line0), (rows1, line1) in zip(refs[-2:], first, second):
        capacity = rows0.shape[0]
        out[0:capacity, :] = rows0
        out[capacity : 2 * capacity, :] = rows1
        out[2 * capacity : 2 * capacity + HEAD, :] = jnp.where(
            _iota((HEAD, line0.shape[1]), 0) == 0, line0, line1
        ).astype(jnp.bfloat16)


def _labels(line):
    line = line.astype(jnp.float32)
    capacity = line.shape[1] // 2
    return (line[:, :capacity] + 256.0 * line[:, capacity:]).astype(jnp.int32) - 1


def _parts(block):
    capacity = block.shape[1] // 2
    head = block[2 * capacity :, :].astype(jnp.float32)
    return [
        (block[i * capacity : (i + 1) * capacity, :], _labels(head[i : i + 1, :]))
        for i in range(2)
    ]


def _totals(blocks, lists):
    parts = [p for b in blocks for p in _parts(b)]
    rows = jnp.concatenate([r for r, _ in parts], axis=0)
    labels = jnp.concatenate([l for _, l in parts], axis=1)
    hot = (_iota((lists, rows.shape[0]), 0) == labels).astype(jnp.float32)
    sums = jnp.dot(hot.astype(jnp.bfloat16), rows, preferred_element_type=jnp.float32)
    return sums, jnp.sum(hot, axis=1, keepdims=True)


def _sums_kernel(*refs):
    *before, a, b, side_a, side_b, out, pack = refs
    lists, width = out.shape[0] - 8, out.shape[1]
    mine, mine_n = _totals((a, b), lists)
    side, side_n = _totals((side_a, side_b), lists)
    count = mine_n + side_n
    eye = _iota((width, width), 0) == _iota((width, width), 1)
    row = _iota((8, width), 0)
    lines = jnp.zeros((8, width), jnp.float32)
    for i in range(lists // width):
        line = jnp.where(eye, count[i * width : (i + 1) * width, :], 0.0)
        lines = jnp.where(row == i, jnp.sum(line, axis=0, keepdims=True), lines)
    if before:
        out[0:lists, :] = before[0][0:lists, :] + (mine + side)
        out[lists:, :] = before[0][lists:, :] + lines
    else:
        out[0:lists, :] = mine + side
        out[lists:, :] = lines
    capacity = width // 2
    lines = []
    for i, block in enumerate((a, b)):
        rows = jnp.where(_core() == 0, block[capacity : 2 * capacity, :], block[0:capacity, :])
        pack[i * capacity : (i + 1) * capacity, :] = rows
        head = block[2 * capacity :, :].astype(jnp.float32)
        lines.append(jnp.where(_core() == 0, head[1:2, :], head[0:1, :]))
    pack[2 * capacity :, :] = jnp.where(
        _iota((HEAD, width), 0) == 0, lines[0], lines[1]
    ).astype(jnp.bfloat16)


def _hot(labels, lists):
    capacity = labels.shape[1]
    eye = _iota((capacity, capacity), 0) == _iota((capacity, capacity), 1)
    column = jnp.sum(
        jnp.where(eye, labels.astype(jnp.float32), 0.0), axis=1, keepdims=True
    ).astype(jnp.int32)
    return _bf16(_iota((capacity, lists), 1) == column)


def _own_part(block):
    (rows0, labels0), (rows1, labels1) = _parts(block)
    return jnp.where(_core() == 0, rows0, rows1), jnp.where(_core() == 0, labels0, labels1)


def _hot_kernel(*refs):
    (*blocks, out) = refs
    capacity = blocks[0].shape[1] // 2
    for i, block in enumerate(blocks):
        out[i * capacity : (i + 1) * capacity, :] = _hot(_own_part(block)[1], out.shape[1])


def _codes_kernel(mine, other, old, hots, *refs):
    (*blocks, fresh, codes, scales) = refs
    lists, width = fresh.shape
    capacity = width // 2
    me, core = lax.axis_index("items"), _core()
    wide = _iota((width, width), 0) == _iota((width, width), 1)
    for i in range(lists // width):
        row = mine[lists + i : lists + i + 1, :] + other[lists + i : lists + i + 1, :]
        counts = jnp.sum(jnp.where(wide, row, 0.0), axis=1, keepdims=True)
        at_i = slice(i * width, (i + 1) * width)
        total = mine[at_i, :] + other[at_i, :] + old[at_i, :].astype(jnp.float32)
        fresh[at_i, :] = (total / (counts + 1.0)).astype(jnp.bfloat16)
    table = fresh[...]
    eye = _iota((capacity, capacity), 0) == _iota((capacity, capacity), 1)
    ordered = []
    for i, (a, b, pack) in enumerate((blocks[0:3], blocks[3:6])):
        base = me ^ (4 * i)
        for j, (block, k) in enumerate(zip((a, b), _owners())):
            at = (2 * i + j) * capacity
            ordered.append((base ^ k, _own_part(block)[0], hots[at : at + capacity, :]))
        for (rows, labels), k in zip(_parts(pack), (core, 3 - core)):
            ordered.append((base ^ k, rows, _hot(labels, lists)))
    for source, rows, hot in ordered:
        lookup = jnp.dot(hot, table, preferred_element_type=jnp.float32)
        residual = rows.astype(jnp.float32) - lookup
        amax = jnp.max(jnp.abs(residual), axis=1, keepdims=True)
        codes[pl.ds(pl.multiple_of(source * capacity, capacity), capacity), :] = (
            residual * (127.0 / (amax + 1e-06))
        ).astype(jnp.bfloat16)
        scales[pl.ds(source, 1), :] = jnp.sum(
            jnp.where(eye, amax / 127.0, 0.0), axis=0, keepdims=True
        )


def _call(kernel, outs, args, flops=0, **options):
    moved = sum(a.size * a.dtype.itemsize for a in args) + sum(
        o.size * o.dtype.itemsize for o in outs
    )
    limit = options.pop("limit", 24 * 2**20)
    return pl.pallas_call(
        kernel,
        out_shape=outs,
        in_specs=[VMEM] * len(args),
        out_specs=[VMEM] * len(outs),
        compiler_params=pltpu.CompilerParams(vmem_limit_bytes=limit),
        cost_estimate=pl.CostEstimate(flops=flops, bytes_accessed=moved, transcendentals=0),
        **options,
    )(*args)


def per_device_eight(embeds, assign, list_slot, old_centroids):
    list_dev, width = old_centroids.shape
    item_dev = embeds.shape[0]
    peers, reps = lax.axis_size("items"), lax.axis_size("rep")
    capacity = 4 * item_dev // peers

    def hop(a, items, rep=0):
        swap = items * reps + rep
        return lax.ppermute(a, ("items", "rep"), [(i, i ^ swap) for i in range(peers * reps)])

    table = list_slot.reshape(-1, 128)
    pair = jax.ShapeDtypeStruct((2 * capacity + HEAD, width), jnp.bfloat16)
    total = jax.ShapeDtypeStruct((list_dev + 8, width), jnp.float32)
    flops = 2 * 4 * capacity * item_dev * width

    def spread(a, items, rep):
        swap = [x * reps + rep for x in items]
        return lax.ppermute(a, ("items", "rep"), [(i, i ^ swap[i & 1]) for i in range(peers * reps)])

    def to_owners(payload, extra, *after):
        wide = jax.ShapeDtypeStruct((pair.shape[0] + extra, width), jnp.bfloat16)
        a, b = _call(
            lambda *refs: _split_kernel(list_dev, *refs),
            [wide] * 2,
            (payload, hop(payload, 0, 1), table, *after),
            flops=flops,
        )
        side_b, near_b = spread(b, (2, 3), 2), spread(b, (2, 3), 0)
        side_a, near_a = spread(a, (1, 0), 2), spread(a, (1, 0), 0)
        return near_a, near_b, side_a, side_b

    payload = lax.optimization_barrier(jnp.pad(embeds, ((0, HEAD), (0, 0))))
    (payload,) = _call(
        _ids_kernel,
        [jax.ShapeDtypeStruct(payload.shape, payload.dtype)],
        (assign.reshape(1, item_dev), payload),
        input_output_aliases={1: 0},
    )
    far = hop(payload, 4)
    near = to_owners(payload, HEAD)
    away = to_owners(far, 0, near[2])
    flops = 2 * list_dev * capacity * width
    mine, near_pack = _call(_sums_kernel, [total, pair], near, flops=8 * flops)
    near_pack = hop(near_pack, 0, 1)
    mine, away_pack = _call(_sums_kernel, [total, pair], (mine, *away), flops=8 * flops)
    away_pack = hop(away_pack, 0, 1)
    other = hop(mine, 0, 1)
    own = (*near[0:2], *away[0:2])
    (hots,) = _call(
        _hot_kernel, [jax.ShapeDtypeStruct((4 * capacity, list_dev), jnp.bfloat16)], own
    )
    fresh, codes, scales = _call(
        _codes_kernel,
        [
            jax.ShapeDtypeStruct((list_dev, width), jnp.bfloat16),
            jax.ShapeDtypeStruct((peers * capacity, width), jnp.bfloat16),
            jax.ShapeDtypeStruct((peers, capacity), jnp.float32),
        ],
        (mine, other, old_centroids, hots, *near[0:2], near_pack, *away[0:2], away_pack),
        flops=8 * flops,
    )
    return (
        fresh,
        codes.reshape(1, 1, peers * capacity, width),
        scales.reshape(1, 1, peers * capacity),
    )


def per_device(embeds, assign, list_slot, old_centroids):
    peers = lax.axis_size("items")
    list_dev = old_centroids.shape[0]
    width = embeds.shape[1]
    item_dev = embeds.shape[0]
    capacity = 4 * item_dev // peers
    slot = list_slot[assign]
    owner = slot // list_dev
    local = slot % list_dev
    member = (owner[:, None] == jnp.arange(peers, dtype=jnp.int32)[None, :]).astype(jnp.int32)
    rank = jnp.sum(member * (jnp.cumsum(member, axis=0) - 1), axis=1)
    target = owner * capacity + rank
    outgoing = jnp.zeros((peers * capacity, width), jnp.bfloat16).at[target].set(embeds)
    labels = jnp.full((peers * capacity,), -1, jnp.int32).at[target].set(local)
    arrived, arrived_ids = (
        lax.all_to_all(
            outgoing.reshape(peers, capacity, width),
            "items",
            split_axis=0,
            concat_axis=0,
            tiled=True,
        ),
        lax.all_to_all(
            labels.reshape(peers, capacity), "items", split_axis=0, concat_axis=0, tiled=True
        ),
    )
    arrived = arrived.reshape(peers * capacity, width)
    arrived_ids = arrived_ids.reshape(peers * capacity)
    member_t = (jnp.arange(list_dev, dtype=jnp.int32)[:, None] == arrived_ids[None, :]).astype(
        jnp.bfloat16
    )
    partial_sums = jnp.dot(member_t, arrived, preferred_element_type=jnp.float32)
    partial_counts = jnp.sum(member_t, axis=1, dtype=jnp.float32)
    total_sums, total_counts = lax.psum((partial_sums, partial_counts), "rep")
    fresh = (
        (total_sums + old_centroids.astype(jnp.float32)) / (total_counts + 1.0)[:, None]
    ).astype(jnp.bfloat16)
    lookup = lax.dot_general(
        member_t, fresh, (((0,), (0,)), ((), ())), preferred_element_type=jnp.float32
    )
    residual = arrived.astype(jnp.float32) - lookup
    amax = jnp.max(jnp.abs(residual), axis=1)
    codes = (residual * (127.0 / (amax + 1e-06))[:, None]).astype(jnp.bfloat16)
    row_scales = amax / 127.0
    return (
        fresh,
        codes.reshape(1, 1, peers * capacity, width),
        row_scales.reshape(1, 1, peers * capacity),
    )


def solution(mesh):
    in_specs = (P(("items", "rep"), None), P(("items", "rep")), P(), P("items", None))
    out_specs = (P("items", None), P("items", "rep", None, None), P("items", "rep", None))
    small = mesh.shape["items"] == 8 and mesh.shape["rep"] == 4
    return jax.shard_map(
        per_device_eight if small else per_device,
        mesh=mesh,
        in_specs=in_specs,
        out_specs=out_specs,
        check_vma=False,
    )
```

```python
import jax
import jax.numpy as jnp
from jax import lax
from jax.experimental import pallas as pl
from jax.experimental.pallas import tpu as pltpu
from jax.sharding import PartitionSpec as P

HEAD = 16
VMEM = pl.BlockSpec(memory_space=pltpu.VMEM)


def _log2(n):
    return n.bit_length() - 1


def _iota(shape, dim):
    return lax.broadcasted_iota(jnp.int32, shape, dim)


def _bf16(a):
    return a.astype(jnp.float32).astype(jnp.bfloat16)


def _slots(table, assign):
    t, n = table.shape[0], assign.shape[1]
    hot = _bf16(_iota((t, n), 0) == (assign >> 7))
    lane = _iota((128, n), 0) == (assign & 127)

    def pick(part):
        rows = lax.dot_general(
            _bf16(part), hot, (((0,), (0,)), ((), ())), preferred_element_type=jnp.float32
        )
        return jnp.sum(jnp.where(lane, rows, 0.0), axis=0, keepdims=True)

    return (pick(table & 255) + 256.0 * pick(table >> 8)).astype(jnp.int32)


def _core():
    return lax.axis_index("rep") & 1


def _heads(list_dev, me, table, payloads):
    n = payloads[0].shape[0] - HEAD
    low = jnp.concatenate([p[n:, :].astype(jnp.float32) for p in payloads], axis=1)
    slot = _slots(table, (low[0:1, :] + 256.0 * low[1:2, :]).astype(jnp.int32))
    relative = (slot >> _log2(list_dev)) ^ me
    code = (slot & (list_dev - 1)) + 1
    lo, hi = (code & 255).astype(jnp.float32), (code >> 8).astype(jnp.float32)
    member = (_iota((HEAD, low.shape[1]), 0) == relative).astype(jnp.float32)
    at = [slice(i * n, (i + 1) * n) for i in range(len(payloads))]
    before = _bf16(_iota((n, n), 0) < _iota((n, n), 1))
    count = jnp.dot(
        jnp.concatenate([member[:, i] for i in at], axis=0).astype(jnp.bfloat16),
        before,
        preferred_element_type=jnp.float32,
    )
    out = []
    for j, i in enumerate(at):
        rank = jnp.sum(member[:, i] * count[j * HEAD : (j + 1) * HEAD, :], axis=0, keepdims=True)
        out.append((rank.astype(jnp.int32), relative[:, i], lo[:, i], hi[:, i]))
    return out


def _route(head, rows, ks):
    rank, relative, lo, hi = head
    n = rows.shape[0]
    capacity = n // 2
    hot = jnp.concatenate(
        [
            (_iota((capacity, n), 0) == jnp.where(relative == k, rank, -1)).astype(jnp.float32)
            for k in ks
        ],
        axis=0,
    ).astype(jnp.bfloat16)
    moved = jnp.dot(hot, rows, preferred_element_type=jnp.float32).astype(jnp.bfloat16)
    values = jnp.where(_iota((HEAD, n), 0) == 0, lo, hi).astype(jnp.bfloat16)
    labels = lax.dot_general(
        values, hot, (((1,), (1,)), ((), ())), preferred_element_type=jnp.float32
    )
    at = [slice(i * capacity, (i + 1) * capacity) for i in range(len(ks))]
    return [
        (moved[i, :], jnp.concatenate([labels[0:1, i], labels[1:2, i]], axis=1)) for i in at
    ]


def _ids_kernel(assign, _, out):
    lo, hi = (assign[...] & 255).astype(jnp.float32), (assign[...] >> 8).astype(jnp.float32)
    n = assign.shape[1]
    out[n:, :] = jnp.where(_iota((HEAD, n), 0) == 0, lo, hi).astype(jnp.bfloat16)


def _owners():
    return 1 - _core(), 2 + _core()


def _split_kernel(list_dev, payload, twin, table, *refs):
    mine, other = payload[...], twin[...]
    both = jnp.where(_core() == 0, mine, other), jnp.where(_core() == 0, other, mine)
    n = mine.shape[0] - HEAD
    heads = _heads(list_dev, lax.axis_index("items"), table[...], both)
    first, second = (_route(h, p[0:n, :], _owners()) for h, p in zip(heads, both))
    for out, (rows0, line0), (rows1, line1) in zip(refs[-2:], first, second):
        capacity = rows0.shape[0]
        out[0:capacity, :] = rows0
        out[capacity : 2 * capacity, :] = rows1
        first_line = _iota((out.shape[0] - 2 * capacity, line0.shape[1]), 0) == 0
        out[2 * capacity :, :] = jnp.where(first_line, line0, line1).astype(jnp.bfloat16)


def _labels(line):
    line = line.astype(jnp.float32)
    capacity = line.shape[1] // 2
    return (line[:, :capacity] + 256.0 * line[:, capacity:]).astype(jnp.int32) - 1


def _parts(block):
    capacity = block.shape[1] // 2
    head = block[2 * capacity :, :].astype(jnp.float32)
    return [
        (block[i * capacity : (i + 1) * capacity, :], _labels(head[i : i + 1, :]))
        for i in range(2)
    ]


def _totals(blocks, lists):
    parts = [p for b in blocks for p in _parts(b)]
    rows = jnp.concatenate([r for r, _ in parts], axis=0)
    labels = jnp.concatenate([l for _, l in parts], axis=1)
    hot = (_iota((lists, rows.shape[0]), 0) == labels).astype(jnp.float32)
    sums = jnp.dot(hot.astype(jnp.bfloat16), rows, preferred_element_type=jnp.float32)
    return sums, jnp.sum(hot, axis=1, keepdims=True)


def _sums_kernel(*refs):
    *before, a, b, side_a, side_b, out, pack = refs
    lists, width = out.shape[0] - 8, out.shape[1]
    mine, mine_n = _totals((a, b), lists)
    side, side_n = _totals((side_a, side_b), lists)
    count = mine_n + side_n
    eye = _iota((width, width), 0) == _iota((width, width), 1)
    row = _iota((8, width), 0)
    lines = jnp.zeros((8, width), jnp.float32)
    for i in range(lists // width):
        line = jnp.where(eye, count[i * width : (i + 1) * width, :], 0.0)
        lines = jnp.where(row == i, jnp.sum(line, axis=0, keepdims=True), lines)
    if before:
        out[0:lists, :] = before[0][0:lists, :] + (mine + side)
        out[lists:, :] = before[0][lists:, :] + lines
    else:
        out[0:lists, :] = mine + side
        out[lists:, :] = lines
    capacity = width // 2
    lines = []
    for i, block in enumerate((a, b)):
        rows = jnp.where(_core() == 0, block[capacity : 2 * capacity, :], block[0:capacity, :])
        pack[i * capacity : (i + 1) * capacity, :] = rows
        head = block[2 * capacity :, :].astype(jnp.float32)
        lines.append(jnp.where(_core() == 0, head[1:2, :], head[0:1, :]))
    pack[2 * capacity :, :] = jnp.where(
        _iota((HEAD, width), 0) == 0, lines[0], lines[1]
    ).astype(jnp.bfloat16)


def _hot(labels, lists):
    capacity = labels.shape[1]
    eye = _iota((capacity, capacity), 0) == _iota((capacity, capacity), 1)
    column = jnp.sum(
        jnp.where(eye, labels.astype(jnp.float32), 0.0), axis=1, keepdims=True
    ).astype(jnp.int32)
    return _bf16(_iota((capacity, lists), 1) == column)


def _own_part(block):
    (rows0, labels0), (rows1, labels1) = _parts(block)
    return jnp.where(_core() == 0, rows0, rows1), jnp.where(_core() == 0, labels0, labels1)


def _hot_kernel(*refs):
    (*blocks, out) = refs
    capacity = blocks[0].shape[1] // 2
    for i, block in enumerate(blocks):
        out[i * capacity : (i + 1) * capacity, :] = _hot(_own_part(block)[1], out.shape[1])


def _codes_kernel(mine, other, old, hots, *refs):
    (*blocks, fresh, codes, scales) = refs
    lists, width = fresh.shape
    capacity = width // 2
    me, core = lax.axis_index("items"), _core()
    wide = _iota((width, width), 0) == _iota((width, width), 1)
    for i in range(lists // width):
        row = mine[lists + i : lists + i + 1, :] + other[lists + i : lists + i + 1, :]
        counts = jnp.sum(jnp.where(wide, row, 0.0), axis=1, keepdims=True)
        at_i = slice(i * width, (i + 1) * width)
        total = mine[at_i, :] + other[at_i, :] + old[at_i, :].astype(jnp.float32)
        fresh[at_i, :] = (total / (counts + 1.0)).astype(jnp.bfloat16)
    table = fresh[...]
    eye = _iota((capacity, capacity), 0) == _iota((capacity, capacity), 1)
    ordered = []
    for i, (a, b, pack) in enumerate((blocks[0:3], blocks[3:6])):
        base = me ^ (4 * i)
        for j, (block, k) in enumerate(zip((a, b), _owners())):
            at = (2 * i + j) * capacity
            ordered.append((base ^ k, _own_part(block)[0], hots[at : at + capacity, :]))
        for (rows, labels), k in zip(_parts(pack), (core, 3 - core)):
            ordered.append((base ^ k, rows, _hot(labels, lists)))
    for source, rows, hot in ordered:
        lookup = jnp.dot(hot, table, preferred_element_type=jnp.float32)
        residual = rows.astype(jnp.float32) - lookup
        amax = jnp.max(jnp.abs(residual), axis=1, keepdims=True)
        codes[pl.ds(pl.multiple_of(source * capacity, capacity), capacity), :] = (
            residual * (127.0 / (amax + 1e-06))
        ).astype(jnp.bfloat16)
        scales[pl.ds(source, 1), :] = jnp.sum(
            jnp.where(eye, amax / 127.0, 0.0), axis=0, keepdims=True
        )


def _call(kernel, outs, args, flops=0, **options):
    moved = sum(a.size * a.dtype.itemsize for a in args) + sum(
        o.size * o.dtype.itemsize for o in outs
    )
    limit = options.pop("limit", 24 * 2**20)
    return pl.pallas_call(
        kernel,
        out_shape=outs,
        in_specs=[VMEM] * len(args),
        out_specs=[VMEM] * len(outs),
        compiler_params=pltpu.CompilerParams(vmem_limit_bytes=limit),
        cost_estimate=pl.CostEstimate(flops=flops, bytes_accessed=moved, transcendentals=0),
        **options,
    )(*args)


def per_device_eight(embeds, assign, list_slot, old_centroids):
    list_dev, width = old_centroids.shape
    item_dev = embeds.shape[0]
    peers, reps = lax.axis_size("items"), lax.axis_size("rep")
    capacity = 4 * item_dev // peers

    def hop(a, items, rep=0):
        swap = items * reps + rep
        return lax.ppermute(a, ("items", "rep"), [(i, i ^ swap) for i in range(peers * reps)])

    table = list_slot.reshape(-1, 128)
    pair = jax.ShapeDtypeStruct((2 * capacity + HEAD, width), jnp.bfloat16)
    total = jax.ShapeDtypeStruct((list_dev + 8, width), jnp.float32)
    flops = 2 * 4 * capacity * item_dev * width

    def spread(a, items, rep):
        swap = [x * reps + rep for x in items]
        return lax.ppermute(a, ("items", "rep"), [(i, i ^ swap[i & 1]) for i in range(peers * reps)])

    def to_owners(payload, extra, *after):
        wide = jax.ShapeDtypeStruct((pair.shape[0] + extra, width), jnp.bfloat16)
        a, b = _call(
            lambda *refs: _split_kernel(list_dev, *refs),
            [wide] * 2,
            (payload, hop(payload, 0, 1), table, *after),
            flops=flops,
        )
        side_b, near_b = spread(b, (2, 3), 2), spread(b, (2, 3), 0)
        side_a, near_a = spread(a, (1, 0), 2), spread(a, (1, 0), 0)
        return near_a, near_b, side_a, side_b

    payload = lax.optimization_barrier(jnp.pad(embeds, ((0, HEAD), (0, 0))))
    (payload,) = _call(
        _ids_kernel,
        [jax.ShapeDtypeStruct(payload.shape, payload.dtype)],
        (assign.reshape(1, item_dev), payload),
        input_output_aliases={1: 0},
    )
    far = hop(payload, 4)
    near = to_owners(payload, HEAD)
    away = to_owners(far, 0, near[2])
    flops = 2 * list_dev * capacity * width
    mine, near_pack = _call(_sums_kernel, [total, pair], near, flops=8 * flops)
    near_pack = hop(near_pack, 0, 1)
    mine, away_pack = _call(_sums_kernel, [total, pair], (mine, *away), flops=8 * flops)
    away_pack = hop(away_pack, 0, 1)
    other = hop(mine, 0, 1)
    own = (*near[0:2], *away[0:2])
    (hots,) = _call(
        _hot_kernel, [jax.ShapeDtypeStruct((4 * capacity, list_dev), jnp.bfloat16)], own
    )
    fresh, codes, scales = _call(
        _codes_kernel,
        [
            jax.ShapeDtypeStruct((list_dev, width), jnp.bfloat16),
            jax.ShapeDtypeStruct((peers * capacity, width), jnp.bfloat16),
            jax.ShapeDtypeStruct((peers, capacity), jnp.float32),
        ],
        (mine, other, old_centroids, hots, *near[0:2], near_pack, *away[0:2], away_pack),
        flops=8 * flops,
    )
    return (
        fresh,
        codes.reshape(1, 1, peers * capacity, width),
        scales.reshape(1, 1, peers * capacity),
    )


def per_device(embeds, assign, list_slot, old_centroids):
    peers = lax.axis_size("items")
    list_dev = old_centroids.shape[0]
    width = embeds.shape[1]
    item_dev = embeds.shape[0]
    capacity = 4 * item_dev // peers
    slot = list_slot[assign]
    owner = slot // list_dev
    local = slot % list_dev
    member = (owner[:, None] == jnp.arange(peers, dtype=jnp.int32)[None, :]).astype(jnp.int32)
    rank = jnp.sum(member * (jnp.cumsum(member, axis=0) - 1), axis=1)
    target = owner * capacity + rank
    outgoing = jnp.zeros((peers * capacity, width), jnp.bfloat16).at[target].set(embeds)
    labels = jnp.full((peers * capacity,), -1, jnp.int32).at[target].set(local)
    arrived, arrived_ids = (
        lax.all_to_all(
            outgoing.reshape(peers, capacity, width),
            "items",
            split_axis=0,
            concat_axis=0,
            tiled=True,
        ),
        lax.all_to_all(
            labels.reshape(peers, capacity), "items", split_axis=0, concat_axis=0, tiled=True
        ),
    )
    arrived = arrived.reshape(peers * capacity, width)
    arrived_ids = arrived_ids.reshape(peers * capacity)
    member_t = (jnp.arange(list_dev, dtype=jnp.int32)[:, None] == arrived_ids[None, :]).astype(
        jnp.bfloat16
    )
    partial_sums = jnp.dot(member_t, arrived, preferred_element_type=jnp.float32)
    partial_counts = jnp.sum(member_t, axis=1, dtype=jnp.float32)
    total_sums, total_counts = lax.psum((partial_sums, partial_counts), "rep")
    fresh = (
        (total_sums + old_centroids.astype(jnp.float32)) / (total_counts + 1.0)[:, None]
    ).astype(jnp.bfloat16)
    lookup = lax.dot_general(
        member_t, fresh, (((0,), (0,)), ((), ())), preferred_element_type=jnp.float32
    )
    residual = arrived.astype(jnp.float32) - lookup
    amax = jnp.max(jnp.abs(residual), axis=1)
    codes = (residual * (127.0 / (amax + 1e-06))[:, None]).astype(jnp.bfloat16)
    row_scales = amax / 127.0
    return (
        fresh,
        codes.reshape(1, 1, peers * capacity, width),
        row_scales.reshape(1, 1, peers * capacity),
    )


def solution(mesh):
    in_specs = (P(("items", "rep"), None), P(("items", "rep")), P(), P("items", None))
    out_specs = (P("items", None), P("items", "rep", None, None), P("items", "rep", None))
    small = mesh.shape["items"] == 8 and mesh.shape["rep"] == 4
    return jax.shard_map(
        per_device_eight if small else per_device,
        mesh=mesh,
        in_specs=in_specs,
        out_specs=out_specs,
        check_vma=False,
    )
```

```python
import jax
import jax.numpy as jnp
from jax import lax
from jax.experimental import pallas as pl
from jax.experimental.pallas import tpu as pltpu
from jax.sharding import PartitionSpec as P

HEAD = 16
VMEM = pl.BlockSpec(memory_space=pltpu.VMEM)


def _log2(n):
    return n.bit_length() - 1


def _iota(shape, dim):
    return lax.broadcasted_iota(jnp.int32, shape, dim)


def _bf16(a):
    return a.astype(jnp.float32).astype(jnp.bfloat16)


def _slots(table, assign):
    t, n = table.shape[0], assign.shape[1]
    hot = _bf16(_iota((t, n), 0) == (assign >> 7))
    lane = _iota((128, n), 0) == (assign & 127)

    def pick(part):
        rows = lax.dot_general(
            _bf16(part), hot, (((0,), (0,)), ((), ())), preferred_element_type=jnp.float32
        )
        return jnp.sum(jnp.where(lane, rows, 0.0), axis=0, keepdims=True)

    return (pick(table & 255) + 256.0 * pick(table >> 8)).astype(jnp.int32)


def _core():
    return lax.axis_index("rep") & 1


def _heads(list_dev, me, table, payloads):
    n = payloads[0].shape[0] - HEAD
    low = jnp.concatenate([p[n:, :].astype(jnp.float32) for p in payloads], axis=1)
    slot = _slots(table, (low[0:1, :] + 256.0 * low[1:2, :]).astype(jnp.int32))
    relative = (slot >> _log2(list_dev)) ^ me
    code = (slot & (list_dev - 1)) + 1
    lo, hi = (code & 255).astype(jnp.float32), (code >> 8).astype(jnp.float32)
    member = (_iota((HEAD, low.shape[1]), 0) == relative).astype(jnp.float32)
    at = [slice(i * n, (i + 1) * n) for i in range(len(payloads))]
    before = _bf16(_iota((n, n), 0) < _iota((n, n), 1))
    count = jnp.dot(
        jnp.concatenate([member[:, i] for i in at], axis=0).astype(jnp.bfloat16),
        before,
        preferred_element_type=jnp.float32,
    )
    out = []
    for j, i in enumerate(at):
        rank = jnp.sum(member[:, i] * count[j * HEAD : (j + 1) * HEAD, :], axis=0, keepdims=True)
        out.append((rank.astype(jnp.int32), relative[:, i], lo[:, i], hi[:, i]))
    return out


def _route(head, rows, ks):
    rank, relative, lo, hi = head
    n = rows.shape[0]
    capacity = n // 2
    hot = jnp.concatenate(
        [
            (_iota((capacity, n), 0) == jnp.where(relative == k, rank, -1)).astype(jnp.float32)
            for k in ks
        ],
        axis=0,
    ).astype(jnp.bfloat16)
    moved = jnp.dot(hot, rows, preferred_element_type=jnp.float32).astype(jnp.bfloat16)
    values = jnp.where(_iota((HEAD, n), 0) == 0, lo, hi).astype(jnp.bfloat16)
    labels = lax.dot_general(
        values, hot, (((1,), (1,)), ((), ())), preferred_element_type=jnp.float32
    )
    at = [slice(i * capacity, (i + 1) * capacity) for i in range(len(ks))]
    return [
        (moved[i, :], jnp.concatenate([labels[0:1, i], labels[1:2, i]], axis=1)) for i in at
    ]


def _ids_kernel(assign, _, out):
    lo, hi = (assign[...] & 255).astype(jnp.float32), (assign[...] >> 8).astype(jnp.float32)
    n = assign.shape[1]
    out[n:, :] = jnp.where(_iota((HEAD, n), 0) == 0, lo, hi).astype(jnp.bfloat16)


def _owners():
    return 1 - _core(), 2 + _core()


def _split_kernel(list_dev, payload, twin, table, *refs):
    mine, other = payload[...], twin[...]
    both = jnp.where(_core() == 0, mine, other), jnp.where(_core() == 0, other, mine)
    n = mine.shape[0] - HEAD
    heads = _heads(list_dev, lax.axis_index("items"), table[...], both)
    first, second = (_route(h, p[0:n, :], _owners()) for h, p in zip(heads, both))
    for out, (rows0, line0), (rows1, line1) in zip(refs[-2:], first, second):
        capacity = rows0.shape[0]
        out[0:capacity, :] = rows0
        out[capacity : 2 * capacity, :] = rows1
        first_line = _iota((out.shape[0] - 2 * capacity, line0.shape[1]), 0) == 0
        out[2 * capacity :, :] = jnp.where(first_line, line0, line1).astype(jnp.bfloat16)


def _labels(line):
    line = line.astype(jnp.float32)
    capacity = line.shape[1] // 2
    return (line[:, :capacity] + 256.0 * line[:, capacity:]).astype(jnp.int32) - 1


def _parts(block):
    capacity = block.shape[1] // 2
    head = block[2 * capacity :, :].astype(jnp.float32)
    return [
        (block[i * capacity : (i + 1) * capacity, :], _labels(head[i : i + 1, :]))
        for i in range(2)
    ]


def _totals(blocks, lists):
    parts = [p for b in blocks for p in _parts(b)]
    rows = jnp.concatenate([r for r, _ in parts], axis=0)
    labels = jnp.concatenate([l for _, l in parts], axis=1)
    hot = (_iota((lists, rows.shape[0]), 0) == labels).astype(jnp.float32)
    sums = jnp.dot(hot.astype(jnp.bfloat16), rows, preferred_element_type=jnp.float32)
    return sums, jnp.sum(hot, axis=1, keepdims=True)


def _add_sums(*refs):
    *before, a, b, side_a, side_b, out = refs
    lists, width = out.shape[0] - 8, out.shape[1]
    mine, mine_n = _totals((a, b), lists)
    side, side_n = _totals((side_a, side_b), lists)
    count = mine_n + side_n
    eye = _iota((width, width), 0) == _iota((width, width), 1)
    row = _iota((8, width), 0)
    lines = jnp.zeros((8, width), jnp.float32)
    for i in range(lists // width):
        line = jnp.where(eye, count[i * width : (i + 1) * width, :], 0.0)
        lines = jnp.where(row == i, jnp.sum(line, axis=0, keepdims=True), lines)
    if before:
        out[0:lists, :] = before[0][0:lists, :] + (mine + side)
        out[lists:, :] = before[0][lists:, :] + lines
    else:
        out[0:lists, :] = mine + side
        out[lists:, :] = lines


def _near_sums_kernel(a, b, side_a, side_b, out):
    _add_sums(a, b, side_a, side_b, out)


def _away_sums_kernel(before, near_a, near_b, a, b, side_a, side_b, out, pack):
    _add_sums(before, a, b, side_a, side_b, out)
    width = out.shape[1]
    capacity = width // 2
    size = 2 * capacity + HEAD
    for j, pair in enumerate(((near_a, near_b), (a, b))):
        lines = []
        for i, block in enumerate(pair):
            rows = jnp.where(_core() == 0, block[capacity : 2 * capacity, :], block[0:capacity, :])
            at = j * size + i * capacity
            pack[at : at + capacity, :] = rows
            head = block[2 * capacity :, :].astype(jnp.float32)
            lines.append(jnp.where(_core() == 0, head[1:2, :], head[0:1, :]))
        at = j * size + 2 * capacity
        pack[at : at + HEAD, :] = jnp.where(
            _iota((HEAD, width), 0) == 0, lines[0], lines[1]
        ).astype(jnp.bfloat16)


def _hot(labels, lists):
    capacity = labels.shape[1]
    eye = _iota((capacity, capacity), 0) == _iota((capacity, capacity), 1)
    column = jnp.sum(
        jnp.where(eye, labels.astype(jnp.float32), 0.0), axis=1, keepdims=True
    ).astype(jnp.int32)
    return _bf16(_iota((capacity, lists), 1) == column)


def _own_part(block):
    (rows0, labels0), (rows1, labels1) = _parts(block)
    return jnp.where(_core() == 0, rows0, rows1), jnp.where(_core() == 0, labels0, labels1)


def _hot_kernel(*refs):
    (*blocks, out) = refs
    capacity = blocks[0].shape[1] // 2
    for i, block in enumerate(blocks):
        out[i * capacity : (i + 1) * capacity, :] = _hot(_own_part(block)[1], out.shape[1])


def _codes_kernel(mine, other, old, hots, *refs):
    (*blocks, fresh, codes, scales) = refs
    lists, width = fresh.shape
    capacity = width // 2
    me, core = lax.axis_index("items"), _core()
    wide = _iota((width, width), 0) == _iota((width, width), 1)
    for i in range(lists // width):
        row = mine[lists + i : lists + i + 1, :] + other[lists + i : lists + i + 1, :]
        counts = jnp.sum(jnp.where(wide, row, 0.0), axis=1, keepdims=True)
        at_i = slice(i * width, (i + 1) * width)
        total = mine[at_i, :] + other[at_i, :] + old[at_i, :].astype(jnp.float32)
        fresh[at_i, :] = (total / (counts + 1.0)).astype(jnp.bfloat16)
    table = fresh[...]
    eye = _iota((capacity, capacity), 0) == _iota((capacity, capacity), 1)
    ordered = []
    size = 2 * capacity + HEAD
    for i, (a, b) in enumerate((blocks[0:2], blocks[2:4])):
        pack = blocks[4][i * size : (i + 1) * size, :]
        base = me ^ (4 * i)
        for j, (block, k) in enumerate(zip((a, b), _owners())):
            at = (2 * i + j) * capacity
            ordered.append((base ^ k, _own_part(block)[0], hots[at : at + capacity, :]))
        for (rows, labels), k in zip(_parts(pack), (core, 3 - core)):
            ordered.append((base ^ k, rows, _hot(labels, lists)))
    for source, rows, hot in ordered:
        lookup = jnp.dot(hot, table, preferred_element_type=jnp.float32)
        residual = rows.astype(jnp.float32) - lookup
        amax = jnp.max(jnp.abs(residual), axis=1, keepdims=True)
        codes[pl.ds(pl.multiple_of(source * capacity, capacity), capacity), :] = (
            residual * (127.0 / (amax + 1e-06))
        ).astype(jnp.bfloat16)
        scales[pl.ds(source, 1), :] = jnp.sum(
            jnp.where(eye, amax / 127.0, 0.0), axis=0, keepdims=True
        )


def _call(kernel, outs, args, flops=0, **options):
    moved = sum(a.size * a.dtype.itemsize for a in args) + sum(
        o.size * o.dtype.itemsize for o in outs
    )
    limit = options.pop("limit", 24 * 2**20)
    return pl.pallas_call(
        kernel,
        out_shape=outs,
        in_specs=[VMEM] * len(args),
        out_specs=[VMEM] * len(outs),
        compiler_params=pltpu.CompilerParams(vmem_limit_bytes=limit),
        cost_estimate=pl.CostEstimate(flops=flops, bytes_accessed=moved, transcendentals=0),
        **options,
    )(*args)


def per_device_eight(embeds, assign, list_slot, old_centroids):
    list_dev, width = old_centroids.shape
    item_dev = embeds.shape[0]
    peers, reps = lax.axis_size("items"), lax.axis_size("rep")
    capacity = 4 * item_dev // peers

    def hop(a, items, rep=0):
        swap = items * reps + rep
        return lax.ppermute(a, ("items", "rep"), [(i, i ^ swap) for i in range(peers * reps)])

    table = list_slot.reshape(-1, 128)
    pair = jax.ShapeDtypeStruct((2 * capacity + HEAD, width), jnp.bfloat16)
    total = jax.ShapeDtypeStruct((list_dev + 8, width), jnp.float32)
    flops = 2 * 4 * capacity * item_dev * width

    def spread(a, items, rep):
        swap = [x * reps + rep for x in items]
        return lax.ppermute(a, ("items", "rep"), [(i, i ^ swap[i & 1]) for i in range(peers * reps)])

    def to_owners(payload, extra, *after):
        wide = jax.ShapeDtypeStruct((pair.shape[0] + extra, width), jnp.bfloat16)
        a, b = _call(
            lambda *refs: _split_kernel(list_dev, *refs),
            [wide] * 2,
            (payload, hop(payload, 0, 1), table, *after),
            flops=flops,
        )
        side_b, near_b = spread(b, (2, 3), 2), spread(b, (2, 3), 0)
        side_a, near_a = spread(a, (1, 0), 2), spread(a, (1, 0), 0)
        return near_a, near_b, side_a, side_b

    payload = lax.optimization_barrier(jnp.pad(embeds, ((0, HEAD), (0, 0))))
    (payload,) = _call(
        _ids_kernel,
        [jax.ShapeDtypeStruct(payload.shape, payload.dtype)],
        (assign.reshape(1, item_dev), payload),
        input_output_aliases={1: 0},
    )
    far = hop(payload, 4)
    near = to_owners(payload, HEAD)
    away = to_owners(far, 0, near[2])
    flops = 2 * list_dev * capacity * width
    (mine,) = _call(_near_sums_kernel, [total], near, flops=8 * flops)
    packs = jax.ShapeDtypeStruct((2 * pair.shape[0], width), jnp.bfloat16)
    mine, pack = _call(
        _away_sums_kernel, [total, packs], (mine, *near[0:2], *away), flops=8 * flops
    )
    pack = hop(pack, 0, 1)
    other = hop(mine, 0, 1)
    own = (*near[0:2], *away[0:2])
    (hots,) = _call(
        _hot_kernel, [jax.ShapeDtypeStruct((4 * capacity, list_dev), jnp.bfloat16)], own
    )
    fresh, codes, scales = _call(
        _codes_kernel,
        [
            jax.ShapeDtypeStruct((list_dev, width), jnp.bfloat16),
            jax.ShapeDtypeStruct((peers * capacity, width), jnp.bfloat16),
            jax.ShapeDtypeStruct((peers, capacity), jnp.float32),
        ],
        (mine, other, old_centroids, hots, *near[0:2], *away[0:2], pack),
        flops=8 * flops,
    )
    return (
        fresh,
        codes.reshape(1, 1, peers * capacity, width),
        scales.reshape(1, 1, peers * capacity),
    )


def per_device(embeds, assign, list_slot, old_centroids):
    peers = lax.axis_size("items")
    list_dev = old_centroids.shape[0]
    width = embeds.shape[1]
    item_dev = embeds.shape[0]
    capacity = 4 * item_dev // peers
    slot = list_slot[assign]
    owner = slot // list_dev
    local = slot % list_dev
    member = (owner[:, None] == jnp.arange(peers, dtype=jnp.int32)[None, :]).astype(jnp.int32)
    rank = jnp.sum(member * (jnp.cumsum(member, axis=0) - 1), axis=1)
    target = owner * capacity + rank
    outgoing = jnp.zeros((peers * capacity, width), jnp.bfloat16).at[target].set(embeds)
    labels = jnp.full((peers * capacity,), -1, jnp.int32).at[target].set(local)
    arrived, arrived_ids = (
        lax.all_to_all(
            outgoing.reshape(peers, capacity, width),
            "items",
            split_axis=0,
            concat_axis=0,
            tiled=True,
        ),
        lax.all_to_all(
            labels.reshape(peers, capacity), "items", split_axis=0, concat_axis=0, tiled=True
        ),
    )
    arrived = arrived.reshape(peers * capacity, width)
    arrived_ids = arrived_ids.reshape(peers * capacity)
    member_t = (jnp.arange(list_dev, dtype=jnp.int32)[:, None] == arrived_ids[None, :]).astype(
        jnp.bfloat16
    )
    partial_sums = jnp.dot(member_t, arrived, preferred_element_type=jnp.float32)
    partial_counts = jnp.sum(member_t, axis=1, dtype=jnp.float32)
    total_sums, total_counts = lax.psum((partial_sums, partial_counts), "rep")
    fresh = (
        (total_sums + old_centroids.astype(jnp.float32)) / (total_counts + 1.0)[:, None]
    ).astype(jnp.bfloat16)
    lookup = lax.dot_general(
        member_t, fresh, (((0,), (0,)), ((), ())), preferred_element_type=jnp.float32
    )
    residual = arrived.astype(jnp.float32) - lookup
    amax = jnp.max(jnp.abs(residual), axis=1)
    codes = (residual * (127.0 / (amax + 1e-06))[:, None]).astype(jnp.bfloat16)
    row_scales = amax / 127.0
    return (
        fresh,
        codes.reshape(1, 1, peers * capacity, width),
        row_scales.reshape(1, 1, peers * capacity),
    )


def solution(mesh):
    in_specs = (P(("items", "rep"), None), P(("items", "rep")), P(), P("items", None))
    out_specs = (P("items", None), P("items", "rep", None, None), P("items", "rep", None))
    small = mesh.shape["items"] == 8 and mesh.shape["rep"] == 4
    return jax.shard_map(
        per_device_eight if small else per_device,
        mesh=mesh,
        in_specs=in_specs,
        out_specs=out_specs,
        check_vma=False,
    )
```

```python
import jax
import jax.numpy as jnp
from jax import lax
from jax.experimental import pallas as pl
from jax.experimental.pallas import tpu as pltpu
from jax.sharding import PartitionSpec as P

HEAD = 16
VMEM = pl.BlockSpec(memory_space=pltpu.VMEM)


def _log2(n):
    return n.bit_length() - 1


def _iota(shape, dim):
    return lax.broadcasted_iota(jnp.int32, shape, dim)


def _bf16(a):
    return a.astype(jnp.float32).astype(jnp.bfloat16)


def _slots(table, assign):
    t, n = table.shape[0], assign.shape[1]
    hot = _bf16(_iota((t, n), 0) == (assign >> 7))
    lane = _iota((128, n), 0) == (assign & 127)

    parts = _bf16(jnp.concatenate([table & 255, table >> 8], axis=1))
    rows = lax.dot_general(
        parts, hot, (((0,), (0,)), ((), ())), preferred_element_type=jnp.float32
    )
    whole = rows[:128, :] + 256.0 * rows[128:, :]
    return jnp.sum(jnp.where(lane, whole, 0.0), axis=0, keepdims=True).astype(jnp.int32)


def _core():
    return lax.axis_index("rep") & 1


def _heads(list_dev, me, table, payloads):
    n = payloads[0].shape[0] - HEAD
    low = jnp.concatenate([p[n:, :].astype(jnp.float32) for p in payloads], axis=1)
    slot = _slots(table, (low[0:1, :] + 256.0 * low[1:2, :]).astype(jnp.int32))
    relative = (slot >> _log2(list_dev)) ^ me
    code = (slot & (list_dev - 1)) + 1
    lo, hi = (code & 255).astype(jnp.float32), (code >> 8).astype(jnp.float32)
    member = (_iota((HEAD, low.shape[1]), 0) == relative).astype(jnp.float32)
    at = [slice(i * n, (i + 1) * n) for i in range(len(payloads))]
    before = _bf16(_iota((n, n), 0) < _iota((n, n), 1))
    count = jnp.dot(
        jnp.concatenate([member[:, i] for i in at], axis=0).astype(jnp.bfloat16),
        before,
        preferred_element_type=jnp.float32,
    )
    out = []
    for j, i in enumerate(at):
        rank = jnp.sum(member[:, i] * count[j * HEAD : (j + 1) * HEAD, :], axis=0, keepdims=True)
        out.append((rank.astype(jnp.int32), relative[:, i], lo[:, i], hi[:, i]))
    return out


def _route(head, rows, ks):
    rank, relative, lo, hi = head
    n = rows.shape[0]
    capacity = n // 2
    hot = jnp.concatenate(
        [
            (_iota((capacity, n), 0) == jnp.where(relative == k, rank, -1)).astype(jnp.float32)
            for k in ks
        ],
        axis=0,
    ).astype(jnp.bfloat16)
    moved = jnp.dot(hot, rows, preferred_element_type=jnp.float32).astype(jnp.bfloat16)
    values = jnp.where(_iota((HEAD, n), 0) == 0, lo, hi).astype(jnp.bfloat16)
    labels = lax.dot_general(
        values, hot, (((1,), (1,)), ((), ())), preferred_element_type=jnp.float32
    )
    at = [slice(i * capacity, (i + 1) * capacity) for i in range(len(ks))]
    return [
        (moved[i, :], jnp.concatenate([labels[0:1, i], labels[1:2, i]], axis=1)) for i in at
    ]


def _ids_kernel(assign, _, out):
    lo, hi = (assign[...] & 255).astype(jnp.float32), (assign[...] >> 8).astype(jnp.float32)
    n = assign.shape[1]
    out[n:, :] = jnp.where(_iota((HEAD, n), 0) == 0, lo, hi).astype(jnp.bfloat16)


def _owners():
    return 1 - _core(), 2 + _core()


def _split_kernel(list_dev, payload, twin, table, *refs):
    mine, other = payload[...], twin[...]
    both = jnp.where(_core() == 0, mine, other), jnp.where(_core() == 0, other, mine)
    n = mine.shape[0] - HEAD
    heads = _heads(list_dev, lax.axis_index("items"), table[...], both)
    first, second = (_route(h, p[0:n, :], _owners()) for h, p in zip(heads, both))
    for out, (rows0, line0), (rows1, line1) in zip(refs[-2:], first, second):
        capacity = rows0.shape[0]
        out[0:capacity, :] = rows0
        out[capacity : 2 * capacity, :] = rows1
        first_line = _iota((out.shape[0] - 2 * capacity, line0.shape[1]), 0) == 0
        out[2 * capacity :, :] = jnp.where(first_line, line0, line1).astype(jnp.bfloat16)


def _labels(line):
    line = line.astype(jnp.float32)
    capacity = line.shape[1] // 2
    return (line[:, :capacity] + 256.0 * line[:, capacity:]).astype(jnp.int32) - 1


def _parts(block):
    capacity = block.shape[1] // 2
    head = block[2 * capacity :, :].astype(jnp.float32)
    return [
        (block[i * capacity : (i + 1) * capacity, :], _labels(head[i : i + 1, :]))
        for i in range(2)
    ]


def _totals(blocks, lists):
    parts = [p for b in blocks for p in _parts(b)]
    rows = jnp.concatenate([r for r, _ in parts], axis=0)
    labels = jnp.concatenate([l for _, l in parts], axis=1)
    hot = (_iota((lists, rows.shape[0]), 0) == labels).astype(jnp.float32)
    sums = jnp.dot(hot.astype(jnp.bfloat16), rows, preferred_element_type=jnp.float32)
    return sums, jnp.sum(hot, axis=1, keepdims=True)


def _sums_kernel(*refs):
    *before, a, b, side_a, side_b, out, pack = refs
    lists, width = out.shape[0] - 8, out.shape[1]
    mine, mine_n = _totals((a, b), lists)
    side, side_n = _totals((side_a, side_b), lists)
    count = mine_n + side_n
    eye = _iota((width, width), 0) == _iota((width, width), 1)
    row = _iota((8, width), 0)
    lines = jnp.zeros((8, width), jnp.float32)
    for i in range(lists // width):
        line = jnp.where(eye, count[i * width : (i + 1) * width, :], 0.0)
        lines = jnp.where(row == i, jnp.sum(line, axis=0, keepdims=True), lines)
    if before:
        out[0:lists, :] = before[0][0:lists, :] + (mine + side)
        out[lists:, :] = before[0][lists:, :] + lines
    else:
        out[0:lists, :] = mine + side
        out[lists:, :] = lines
    capacity = width // 2
    lines = []
    for i, block in enumerate((a, b)):
        rows = jnp.where(_core() == 0, block[capacity : 2 * capacity, :], block[0:capacity, :])
        pack[i * capacity : (i + 1) * capacity, :] = rows
        head = block[2 * capacity :, :].astype(jnp.float32)
        lines.append(jnp.where(_core() == 0, head[1:2, :], head[0:1, :]))
    pack[2 * capacity :, :] = jnp.where(
        _iota((HEAD, width), 0) == 0, lines[0], lines[1]
    ).astype(jnp.bfloat16)


def _hot(labels, lists):
    capacity = labels.shape[1]
    eye = _iota((capacity, capacity), 0) == _iota((capacity, capacity), 1)
    column = jnp.sum(
        jnp.where(eye, labels.astype(jnp.float32), 0.0), axis=1, keepdims=True
    ).astype(jnp.int32)
    return _bf16(_iota((capacity, lists), 1) == column)


def _own_part(block):
    (rows0, labels0), (rows1, labels1) = _parts(block)
    return jnp.where(_core() == 0, rows0, rows1), jnp.where(_core() == 0, labels0, labels1)


def _hot_kernel(*refs):
    (*blocks, out) = refs
    capacity = blocks[0].shape[1] // 2
    for i, block in enumerate(blocks):
        out[i * capacity : (i + 1) * capacity, :] = _hot(_own_part(block)[1], out.shape[1])


def _codes_kernel(mine, other, old, hots, *refs):
    (*blocks, fresh, codes, scales) = refs
    lists, width = fresh.shape
    capacity = width // 2
    me, core = lax.axis_index("items"), _core()
    wide = _iota((width, width), 0) == _iota((width, width), 1)
    for i in range(lists // width):
        row = mine[lists + i : lists + i + 1, :] + other[lists + i : lists + i + 1, :]
        counts = jnp.sum(jnp.where(wide, row, 0.0), axis=1, keepdims=True)
        at_i = slice(i * width, (i + 1) * width)
        total = mine[at_i, :] + other[at_i, :] + old[at_i, :].astype(jnp.float32)
        fresh[at_i, :] = (total / (counts + 1.0)).astype(jnp.bfloat16)
    table = fresh[...]
    eye = _iota((capacity, capacity), 0) == _iota((capacity, capacity), 1)
    ordered = []
    for i, (a, b, pack) in enumerate((blocks[0:3], blocks[3:6])):
        base = me ^ (4 * i)
        for j, (block, k) in enumerate(zip((a, b), _owners())):
            at = (2 * i + j) * capacity
            ordered.append((base ^ k, _own_part(block)[0], hots[at : at + capacity, :]))
        for (rows, labels), k in zip(_parts(pack), (core, 3 - core)):
            ordered.append((base ^ k, rows, _hot(labels, lists)))
    for source, rows, hot in ordered:
        lookup = jnp.dot(hot, table, preferred_element_type=jnp.float32)
        residual = rows.astype(jnp.float32) - lookup
        amax = jnp.max(jnp.abs(residual), axis=1, keepdims=True)
        codes[pl.ds(pl.multiple_of(source * capacity, capacity), capacity), :] = (
            residual * (127.0 / (amax + 1e-06))
        ).astype(jnp.bfloat16)
        scales[pl.ds(source, 1), :] = jnp.sum(
            jnp.where(eye, amax / 127.0, 0.0), axis=0, keepdims=True
        )


def _call(kernel, outs, args, flops=0, **options):
    moved = sum(a.size * a.dtype.itemsize for a in args) + sum(
        o.size * o.dtype.itemsize for o in outs
    )
    limit = options.pop("limit", 24 * 2**20)
    return pl.pallas_call(
        kernel,
        out_shape=outs,
        in_specs=[VMEM] * len(args),
        out_specs=[VMEM] * len(outs),
        compiler_params=pltpu.CompilerParams(vmem_limit_bytes=limit),
        cost_estimate=pl.CostEstimate(flops=flops, bytes_accessed=moved, transcendentals=0),
        **options,
    )(*args)


def per_device_eight(embeds, assign, list_slot, old_centroids):
    list_dev, width = old_centroids.shape
    item_dev = embeds.shape[0]
    peers, reps = lax.axis_size("items"), lax.axis_size("rep")
    capacity = 4 * item_dev // peers

    def hop(a, items, rep=0):
        swap = items * reps + rep
        return lax.ppermute(a, ("items", "rep"), [(i, i ^ swap) for i in range(peers * reps)])

    table = list_slot.reshape(-1, 128)
    pair = jax.ShapeDtypeStruct((2 * capacity + HEAD, width), jnp.bfloat16)
    total = jax.ShapeDtypeStruct((list_dev + 8, width), jnp.float32)
    flops = 2 * 4 * capacity * item_dev * width

    def spread(a, items, rep):
        swap = [x * reps + rep for x in items]
        return lax.ppermute(a, ("items", "rep"), [(i, i ^ swap[i & 1]) for i in range(peers * reps)])

    def to_owners(payload, extra, *after):
        wide = jax.ShapeDtypeStruct((pair.shape[0] + extra, width), jnp.bfloat16)
        a, b = _call(
            lambda *refs: _split_kernel(list_dev, *refs),
            [wide] * 2,
            (payload, hop(payload, 0, 1), table, *after),
            flops=flops,
        )
        side_b, near_b = spread(b, (2, 3), 2), spread(b, (2, 3), 0)
        side_a, near_a = spread(a, (1, 0), 2), spread(a, (1, 0), 0)
        return near_a, near_b, side_a, side_b

    payload = lax.optimization_barrier(jnp.pad(embeds, ((0, HEAD), (0, 0))))
    (payload,) = _call(
        _ids_kernel,
        [jax.ShapeDtypeStruct(payload.shape, payload.dtype)],
        (assign.reshape(1, item_dev), payload),
        input_output_aliases={1: 0},
    )
    far = hop(payload, 4)
    near = to_owners(payload, HEAD)
    away = to_owners(far, 0, near[2])
    flops = 2 * list_dev * capacity * width
    mine, near_pack = _call(_sums_kernel, [total, pair], near, flops=8 * flops)
    near_pack = hop(near_pack, 0, 1)
    mine, away_pack = _call(_sums_kernel, [total, pair], (mine, *away), flops=8 * flops)
    away_pack = hop(away_pack, 0, 1)
    other = hop(mine, 0, 1)
    own = (*near[0:2], *away[0:2])
    (hots,) = _call(
        _hot_kernel, [jax.ShapeDtypeStruct((4 * capacity, list_dev), jnp.bfloat16)], own
    )
    fresh, codes, scales = _call(
        _codes_kernel,
        [
            jax.ShapeDtypeStruct((list_dev, width), jnp.bfloat16),
            jax.ShapeDtypeStruct((peers * capacity, width), jnp.bfloat16),
            jax.ShapeDtypeStruct((peers, capacity), jnp.float32),
        ],
        (mine, other, old_centroids, hots, *near[0:2], near_pack, *away[0:2], away_pack),
        flops=8 * flops,
    )
    return (
        fresh,
        codes.reshape(1, 1, peers * capacity, width),
        scales.reshape(1, 1, peers * capacity),
    )


def per_device(embeds, assign, list_slot, old_centroids):
    peers = lax.axis_size("items")
    list_dev = old_centroids.shape[0]
    width = embeds.shape[1]
    item_dev = embeds.shape[0]
    capacity = 4 * item_dev // peers
    slot = list_slot[assign]
    owner = slot // list_dev
    local = slot % list_dev
    member = (owner[:, None] == jnp.arange(peers, dtype=jnp.int32)[None, :]).astype(jnp.int32)
    rank = jnp.sum(member * (jnp.cumsum(member, axis=0) - 1), axis=1)
    target = owner * capacity + rank
    outgoing = jnp.zeros((peers * capacity, width), jnp.bfloat16).at[target].set(embeds)
    labels = jnp.full((peers * capacity,), -1, jnp.int32).at[target].set(local)
    arrived, arrived_ids = (
        lax.all_to_all(
            outgoing.reshape(peers, capacity, width),
            "items",
            split_axis=0,
            concat_axis=0,
            tiled=True,
        ),
        lax.all_to_all(
            labels.reshape(peers, capacity), "items", split_axis=0, concat_axis=0, tiled=True
        ),
    )
    arrived = arrived.reshape(peers * capacity, width)
    arrived_ids = arrived_ids.reshape(peers * capacity)
    member_t = (jnp.arange(list_dev, dtype=jnp.int32)[:, None] == arrived_ids[None, :]).astype(
        jnp.bfloat16
    )
    partial_sums = jnp.dot(member_t, arrived, preferred_element_type=jnp.float32)
    partial_counts = jnp.sum(member_t, axis=1, dtype=jnp.float32)
    total_sums, total_counts = lax.psum((partial_sums, partial_counts), "rep")
    fresh = (
        (total_sums + old_centroids.astype(jnp.float32)) / (total_counts + 1.0)[:, None]
    ).astype(jnp.bfloat16)
    lookup = lax.dot_general(
        member_t, fresh, (((0,), (0,)), ((), ())), preferred_element_type=jnp.float32
    )
    residual = arrived.astype(jnp.float32) - lookup
    amax = jnp.max(jnp.abs(residual), axis=1)
    codes = (residual * (127.0 / (amax + 1e-06))[:, None]).astype(jnp.bfloat16)
    row_scales = amax / 127.0
    return (
        fresh,
        codes.reshape(1, 1, peers * capacity, width),
        row_scales.reshape(1, 1, peers * capacity),
    )


def solution(mesh):
    in_specs = (P(("items", "rep"), None), P(("items", "rep")), P(), P("items", None))
    out_specs = (P("items", None), P("items", "rep", None, None), P("items", "rep", None))
    small = mesh.shape["items"] == 8 and mesh.shape["rep"] == 4
    return jax.shard_map(
        per_device_eight if small else per_device,
        mesh=mesh,
        in_specs=in_specs,
        out_specs=out_specs,
        check_vma=False,
    )
```
